32 devices in a mesh: section: 4 (over y, x), rows: 2 (over core), dp: 4 (over z).
Axes of the slice: x: 2, y: 2, z: 4, core: 2. Of those that a mesh axis runs over, the one named last changes fastest.
Arguments:
- latent: bfloat16 [8, 2, 8, 8, 192], P('dp', None, 'rows'), may hold values from -6 to 6
- enc_weight: bfloat16 [4, 5184, 192], P('section'), may hold values from -0.078125 to 0.078125
- dec_weight: bfloat16 [4, 5184, 192], P('section'), may hold values from -0.078125 to 0.078125
- enc_gain: float32 [4, 192], P('section'), may hold values from 0.1 to 1.9
- dec_gain: float32 [4, 192], P('section'), may hold values from 0.1 to 1.9
- out_grad: bfloat16 [8, 2, 8, 8, 192], P('dp', None, 'rows'), may hold values from -6 to 6
Outputs:
- enc_wgrad: float32 [4, 5184, 192], P('section', ('rows', 'dp'))
- dec_wgrad: float32 [4, 5184, 192], P('section', ('rows', 'dp'))
- enc_ggrad: float32 [4, 192], P('section', ('rows', 'dp'))
- dec_ggrad: float32 [4, 192], P('section', ('rows', 'dp'))
The draws below stay inside these ranges and needn't reach their ends.
All inputs are finite; a program needn't handle non-finite values.
Results may differ from the reference program's by a relative error of at most 0.028.
Values may be sent and summed in bfloat16 or wider, within the bound.
A program may use at most 128 MiB of HBM per device.

```python
import math
import jax
import jax.numpy as jnp
from jax import lax

C = 192
GROUPS = 32
KC = 5184
FR = 2
COLS = 8
HALF = 4
HH = 8
BATCH = 8


def draw_latent(key, part):
    position = jnp.arange(HH, dtype=jnp.float32) / max(HH - 1, 1)
    amplitude = 0.7 * jnp.exp2(position)
    base_vals = jnp.clip(jax.random.normal(key, (BATCH, FR, HH, COLS, C), jnp.float32), -4.0, 4.0)
    return (base_vals * amplitude[None, None, :, None, None]).astype(jnp.bfloat16)


def shard_levels(rng, extent, cuts, least, top_value):
    level = 1.0
    for axis_at, shards_of in cuts:
        draws = jax.random.uniform(jax.random.fold_in(jax.random.fold_in(rng, 6), axis_at), (shards_of,), jnp.float32, least / len(cuts), top_value / len(cuts))
        level = level * jnp.repeat(jnp.exp(draws), extent[axis_at] // shards_of).reshape((-1,) + (1,) * (len(extent) - 1 - axis_at))
    return level


def gaussian(stream_key, extent, scale, most, split=(), held_as=jnp.bfloat16):
    values = jax.random.normal(stream_key, extent, jnp.float32) * scale
    if len(split) > 0:
        values = shard_levels(stream_key, extent, split, -0.22, 0.18) * values
    return jnp.clip(values, min=-most, max=most).astype(held_as)


def setup_inputs(seed: int = 0) -> dict:
    key_list = jax.random.split(jax.random.key(seed), 7)
    return {
        "latent": draw_latent(jax.random.fold_in(key_list[6], 71), 0),
        "enc_weight": gaussian(key_list[1], (HALF, KC, C), KC ** -0.5, 0.078125, ((0, 4),)),
        "dec_weight": gaussian(key_list[2], (HALF, KC, C), KC ** -0.5, 0.078125, ((0, 4),)),
        "enc_gain": jnp.clip(1.0 + 0.18 * jax.random.normal(key_list[3], (HALF, C), jnp.float32), 0.1, 1.9),
        "dec_gain": jnp.clip(1.0 + 0.18 * jax.random.normal(key_list[4], (HALF, C), jnp.float32), 0.1, 1.9),
        "out_grad": gaussian(key_list[5], (BATCH, FR, HH, COLS, C), 1.0, 6.0, ((0, 4), (2, 2))),
    }


EPSILON = 1e-05

def gather_patches(grown_rows):
    frames, padded_rows, columns, channels = grown_rows.shape
    inner_rows = padded_rows - 2
    padded = jnp.pad(grown_rows, ((1, 1), (0, 0), (1, 1), (0, 0)))
    pieces = []
    for lag_frame in range(3):
        for lag_row in range(3):
            for lag_column in range(3):
                pieces.append(padded[lag_frame:lag_frame + frames, lag_row:lag_row + inner_rows, lag_column:lag_column + columns, :])
    return jnp.concatenate(pieces, axis=-1).reshape(frames * inner_rows * columns, 27 * channels)

def convolve(volume, weights):

    def single(sample):
        grown_rows = jnp.pad(sample, ((0, 0), (1, 1), (0, 0), (0, 0)))
        flat_out = jnp.dot(gather_patches(grown_rows), weights, preferred_element_type=jnp.float32)
        return flat_out.reshape(sample.shape[:-1] + (weights.shape[1],))
    return lax.map(single, volume)

def weight_gradient(volume, cotangent):

    def single(summed, paired):
        sample, grad_low = paired
        grown_rows = jnp.pad(sample, ((0, 0), (1, 1), (0, 0), (0, 0)))
        patches = gather_patches(grown_rows)
        product = lax.dot_general(patches, grad_low.reshape(-1, grad_low.shape[-1]), (((0,), (0,)), ((), ())), preferred_element_type=jnp.float32)
        return (summed + product, None)
    initial = jnp.zeros((27 * volume.shape[-1], cotangent.shape[-1]), jnp.float32)
    summed, unused = lax.scan(single, initial, (volume, cotangent))
    return summed

def group_stats(volume):
    batches = volume.shape[0]
    channels = volume.shape[-1]
    grouped = volume.reshape(batches, -1, GROUPS, channels // GROUPS)
    counted = grouped.shape[1] * grouped.shape[3]
    centre = lax.optimization_barrier(jnp.sum(grouped, axis=(1, 3))) / counted
    deviation = grouped - centre[:, None, :, None]
    spread = lax.optimization_barrier(jnp.sum(deviation * deviation, axis=(1, 3))) / counted
    return (centre, lax.rsqrt(spread + EPSILON))

def per_channel(values, channels):
    return jnp.repeat(values, channels // GROUPS, axis=-1)[:, None, None, None, :]

def forward_block(volume, gain_vec, weights):
    channels = volume.shape[-1]
    centre, inverse = group_stats(volume)
    normed = (volume - per_channel(centre, channels)) * per_channel(inverse, channels)
    active = jax.nn.silu(normed * gain_vec).astype(jnp.bfloat16)
    return (active, volume + convolve(active, weights))

def backward_block(volume, gain_vec, weights, active, cotangent):
    channels = volume.shape[-1]
    batches = volume.shape[0]
    centre, inverse = group_stats(volume)
    inverse_full = per_channel(inverse, channels)
    normed = (volume - per_channel(centre, channels)) * inverse_full
    zvalue = normed * gain_vec
    cotangent_low = cotangent.astype(jnp.bfloat16)
    blocks = weights.reshape(27, channels, -1)[::-1]
    reverse_weights = jnp.swapaxes(blocks, 1, 2).reshape(-1, channels)
    act_grad = convolve(cotangent_low, reverse_weights)
    logistic = jax.nn.sigmoid(zvalue)
    pre_grad = act_grad * logistic * (1.0 + zvalue * (1.0 - logistic))
    hat_grad = pre_grad * gain_vec
    grouped_grad = hat_grad.reshape(batches, -1, GROUPS, channels // GROUPS)
    grouped_hat = normed.reshape(batches, -1, GROUPS, channels // GROUPS)
    counted = grouped_grad.shape[1] * grouped_grad.shape[3]
    first_sum = lax.optimization_barrier(jnp.sum(grouped_grad, axis=(1, 3)))
    second_sum = lax.optimization_barrier(jnp.sum(grouped_grad * grouped_hat, axis=(1, 3)))
    input_grad = inverse_full * (hat_grad - per_channel(first_sum / counted, channels) - normed * per_channel(second_sum / counted, channels))
    gain_grad = lax.optimization_barrier(jnp.sum(pre_grad * normed, axis=(0, 1, 2, 3)))
    return (cotangent + input_grad, weight_gradient(active, cotangent_low), gain_grad)

def reference(latent, enc_weight, dec_weight, enc_gain, dec_gain, out_grad):
    hidden = latent
    enc_inputs = []
    enc_active = []
    for level_idx in range(HALF):
        enc_inputs.append(hidden)
        active, result = forward_block(hidden.astype(jnp.float32), enc_gain[level_idx], enc_weight[level_idx])
        enc_active.append(active)
        hidden = result.astype(jnp.bfloat16)
    dec_downs = [None] * HALF
    dec_active = [None] * HALF
    coming = hidden
    for level_idx in reversed(range(HALF)):
        dec_downs[level_idx] = coming
        united = coming.astype(jnp.float32) + enc_inputs[level_idx].astype(jnp.float32)
        active, result = forward_block(united, dec_gain[level_idx], dec_weight[level_idx])
        dec_active[level_idx] = active
        coming = result.astype(jnp.bfloat16)
    loss_scale = 1.0 / math.sqrt(BATCH * FR * HH * COLS)
    cotangent = out_grad.astype(jnp.float32) * loss_scale
    skip_grads = [None] * HALF
    dec_weights_grad = [None] * HALF
    dec_gains_grad = [None] * HALF
    for level_idx in range(HALF):
        united = dec_downs[level_idx].astype(jnp.float32) + enc_inputs[level_idx].astype(jnp.float32)
        cotangent, weight_grad, gain_grad = backward_block(united, dec_gain[level_idx], dec_weight[level_idx], dec_active[level_idx], cotangent)
        skip_grads[level_idx] = cotangent
        dec_weights_grad[level_idx] = weight_grad
        dec_gains_grad[level_idx] = gain_grad
    enc_weights_grad = [None] * HALF
    enc_gains_grad = [None] * HALF
    for level_idx in reversed(range(HALF)):
        passed, weight_grad, gain_grad = backward_block(enc_inputs[level_idx].astype(jnp.float32), enc_gain[level_idx], enc_weight[level_idx], enc_active[level_idx], cotangent)
        cotangent = passed + skip_grads[level_idx]
        enc_weights_grad[level_idx] = weight_grad
        enc_gains_grad[level_idx] = gain_grad
    return (jnp.stack(enc_weights_grad), jnp.stack(dec_weights_grad), jnp.stack(enc_gains_grad), jnp.stack(dec_gains_grad))
```

```python
import functools
import math

import jax
import jax.numpy as jnp
import numpy as np
from jax import lax
from jax.experimental import pallas as pl
from jax.experimental.pallas import tpu as pltpu
from jax.sharding import PartitionSpec as P

GROUPS = 32


EPSILON = 1e-05


def padded_2(block, sides, width):
    for axis, dim in sides:
        count = lax.axis_size(axis)
        forward = [(i, i + 1) for i in range(count - 1)]
        backward = [(target, source) for source, target in forward]
        low = lax.ppermute(
            lax.slice_in_dim(block, block.shape[dim] - width, None, axis=dim), axis, forward
        )
        high = lax.ppermute(lax.slice_in_dim(block, 0, width, axis=dim), axis, backward)
        block = jnp.concatenate([low, block, high], axis=dim)
    return block


def passed_along(block, axis, distance):
    devices = range(lax.axis_size(axis))
    route = [(i - distance, i) for i in devices if i - distance in devices]
    return lax.ppermute(block, axis, route)


def spread_groups(values, channels):
    return jnp.repeat(values, channels // GROUPS)


def gather_patches(grown_rows):
    frames, padded_rows, columns, channels = grown_rows.shape
    inner_rows = padded_rows - 2
    padded = jnp.pad(grown_rows, ((1, 1), (0, 0), (1, 1), (0, 0)))
    pieces = []
    for lag_frame in range(3):
        for lag_row in range(3):
            for lag_column in range(3):
                pieces.append(
                    padded[
                        lag_frame : lag_frame + frames,
                        lag_row : lag_row + inner_rows,
                        lag_column : lag_column + columns,
                        :,
                    ]
                )
    return jnp.concatenate(pieces, axis=-1).reshape(frames * inner_rows * columns, 27 * channels)


def flipped(weights):
    channels = weights.shape[1]
    blocks = weights.reshape(27, -1, channels)[::-1]
    return jnp.swapaxes(blocks, 1, 2).reshape(-1, blocks.shape[1])


def take_slot(buffer, slot_index):
    return lax.dynamic_index_in_dim(buffer, slot_index, 0, keepdims=False)


def store_slot(buffer, slot_index, valid_now, new_value):
    kept = jnp.where(valid_now, new_value, take_slot(buffer, slot_index))
    return lax.dynamic_update_index_in_dim(buffer, kept, slot_index, 0)


def weight_gradient(grown_all, cotangent_all):
    patches = jax.vmap(gather_patches)(grown_all)
    patches = patches.reshape(-1, patches.shape[-1])
    flat_cot = cotangent_all.reshape(-1, cotangent_all.shape[-1])
    return lax.dot_general(
        patches, flat_cot, (((0,), (0,)), ((), ())), preferred_element_type=jnp.float32
    )


def norm_stats(volume, counted):
    grouped = volume.reshape(-1, GROUPS, volume.shape[-1] // GROUPS)
    totals = lax.psum(jnp.sum(grouped, axis=(0, 2)), "rows")
    centre = totals / counted
    deviation = grouped - centre[None, :, None]
    spread = lax.psum(jnp.sum(deviation * deviation, axis=(0, 2)), "rows") / counted
    return (centre, lax.rsqrt(spread + EPSILON))


def forward_block(volume, gain_vec, weights, counted):
    channels = volume.shape[-1]
    centre, inverse = norm_stats(volume, counted)
    normed = (volume - spread_groups(centre, channels)) * spread_groups(inverse, channels)
    active = jax.nn.silu(normed * gain_vec).astype(jnp.bfloat16)
    grown_act = padded_2(active, (("rows", 1),), 1)
    conv_out = jnp.dot(gather_patches(grown_act), weights, preferred_element_type=jnp.float32)
    return (grown_act, centre, inverse, volume + conv_out.reshape(volume.shape))


def backward_block(volume, gain_vec, reverse_weights, centre, inverse, cotangent, counted):
    channels = volume.shape[-1]
    inverse_full = spread_groups(inverse, channels)
    normed = (volume - spread_groups(centre, channels)) * inverse_full
    zvalue = normed * gain_vec
    cotangent_low = cotangent.astype(jnp.bfloat16)
    grown_cot = padded_2(cotangent_low, (("rows", 1),), 1)
    act_grad = jnp.dot(
        gather_patches(grown_cot), reverse_weights, preferred_element_type=jnp.float32
    ).reshape(volume.shape)
    logistic = jax.nn.sigmoid(zvalue)
    pre_grad = act_grad * logistic * (1.0 + zvalue * (1.0 - logistic))
    hat_grad = pre_grad * gain_vec
    grouped_grad = hat_grad.reshape(-1, GROUPS, channels // GROUPS)
    grouped_hat = normed.reshape(-1, GROUPS, channels // GROUPS)
    first_sum, second_sum = lax.psum(
        (jnp.sum(grouped_grad, axis=(0, 2)), jnp.sum(grouped_grad * grouped_hat, axis=(0, 2))),
        "rows",
    )
    input_grad = inverse_full * (
        hat_grad
        - spread_groups(first_sum / counted, channels)
        - normed * spread_groups(second_sum / counted, channels)
    )
    gain_part = jnp.sum((pre_grad * normed).reshape(-1, channels), axis=0)
    return (cotangent + input_grad, cotangent_low, gain_part)


def on_device(latent, enc_weight, dec_weight, enc_gain, dec_gain, out_grad):
    section_pos = lax.axis_index("section")
    section_count = lax.axis_size("section")
    batches, frames, rows_here, columns, channels = latent.shape
    counted = frames * rows_here * columns * (channels // GROUPS) * lax.axis_size("rows")
    cells_all = batches * lax.axis_size("dp") * frames * rows_here * lax.axis_size("rows") * columns
    loss_scale = 1.0 / math.sqrt(cells_all)
    clock_len = batches + section_count - 1
    last_pos = section_count - 1
    grown_shape = (batches, frames, rows_here + 2, columns, channels)
    enc_inputs = jnp.zeros(latent.shape, jnp.bfloat16)
    enc_tops = jnp.zeros(latent.shape, jnp.bfloat16)
    enc_grown = jnp.zeros(grown_shape, jnp.bfloat16)
    enc_centre = jnp.zeros((batches, GROUPS), jnp.float32)
    enc_inverse = jnp.zeros((batches, GROUPS), jnp.float32)
    arriving = jnp.zeros(latent.shape[1:], jnp.bfloat16)
    for clock_step in range(clock_len):
        micro_index = clock_step - section_pos
        valid_now = (micro_index >= 0) & (micro_index < batches)
        slot_index = jnp.clip(micro_index, 0, batches - 1)
        entering = jnp.where(section_pos == 0, latent[min(clock_step, batches - 1)], arriving)
        grown_act, centre, inverse, result = forward_block(
            entering.astype(jnp.float32), enc_gain[0], enc_weight[0], counted
        )
        leaving = result.astype(jnp.bfloat16)
        enc_inputs = store_slot(enc_inputs, slot_index, valid_now, entering)
        enc_tops = store_slot(enc_tops, slot_index, valid_now, leaving)
        enc_grown = store_slot(enc_grown, slot_index, valid_now, grown_act)
        enc_centre = store_slot(enc_centre, slot_index, valid_now, centre)
        enc_inverse = store_slot(enc_inverse, slot_index, valid_now, inverse)
        if clock_step + 1 < clock_len:
            arriving = passed_along(leaving, "section", 1)
    dec_downs = jnp.zeros(latent.shape, jnp.bfloat16)
    dec_grown = jnp.zeros(grown_shape, jnp.bfloat16)
    dec_centre = jnp.zeros((batches, GROUPS), jnp.float32)
    dec_inverse = jnp.zeros((batches, GROUPS), jnp.float32)
    arriving = jnp.zeros(latent.shape[1:], jnp.bfloat16)
    for clock_step in range(clock_len):
        micro_index = clock_step - (last_pos - section_pos)
        valid_now = (micro_index >= 0) & (micro_index < batches)
        slot_index = jnp.clip(micro_index, 0, batches - 1)
        coming = jnp.where(section_pos == last_pos, take_slot(enc_tops, slot_index), arriving)
        united = coming.astype(jnp.float32) + take_slot(enc_inputs, slot_index).astype(jnp.float32)
        grown_act, centre, inverse, result = forward_block(
            united, dec_gain[0], dec_weight[0], counted
        )
        dec_downs = store_slot(dec_downs, slot_index, valid_now, coming)
        dec_grown = store_slot(dec_grown, slot_index, valid_now, grown_act)
        dec_centre = store_slot(dec_centre, slot_index, valid_now, centre)
        dec_inverse = store_slot(dec_inverse, slot_index, valid_now, inverse)
        if clock_step + 1 < clock_len:
            arriving = passed_along(result.astype(jnp.bfloat16), "section", -1)
    dec_reverse = flipped(dec_weight[0])
    skip_grads = jnp.zeros(latent.shape, jnp.float32)
    dec_cotangents = jnp.zeros(latent.shape, jnp.bfloat16)
    dec_gain_sum = jnp.zeros((channels,), jnp.float32)
    arriving_grad = jnp.zeros(latent.shape[1:], jnp.float32)
    for clock_step in range(clock_len):
        micro_index = clock_step - section_pos
        valid_now = (micro_index >= 0) & (micro_index < batches)
        slot_index = jnp.clip(micro_index, 0, batches - 1)
        seeded = out_grad[min(clock_step, batches - 1)].astype(jnp.float32) * loss_scale
        incoming = jnp.where(valid_now, jnp.where(section_pos == 0, seeded, arriving_grad), 0.0)
        united = take_slot(dec_downs, slot_index).astype(jnp.float32) + take_slot(
            enc_inputs, slot_index
        ).astype(jnp.float32)
        passed, cotangent_low, gain_part = backward_block(
            united,
            dec_gain[0],
            dec_reverse,
            take_slot(dec_centre, slot_index),
            take_slot(dec_inverse, slot_index),
            incoming,
            counted,
        )
        dec_gain_sum = dec_gain_sum + gain_part
        dec_cotangents = store_slot(dec_cotangents, slot_index, valid_now, cotangent_low)
        skip_grads = store_slot(skip_grads, slot_index, valid_now, passed)
        if clock_step + 1 < clock_len:
            arriving_grad = passed_along(passed.astype(jnp.bfloat16), "section", 1).astype(
                passed.dtype
            )
    dec_gradient = weight_gradient(dec_grown, dec_cotangents)
    enc_reverse = flipped(enc_weight[0])
    enc_cotangents = jnp.zeros(latent.shape, jnp.bfloat16)
    enc_gain_sum = jnp.zeros((channels,), jnp.float32)
    arriving_grad = jnp.zeros(latent.shape[1:], jnp.float32)
    for clock_step in range(clock_len):
        micro_index = clock_step - (last_pos - section_pos)
        valid_now = (micro_index >= 0) & (micro_index < batches)
        slot_index = jnp.clip(micro_index, 0, batches - 1)
        skip_here = take_slot(skip_grads, slot_index)
        incoming = jnp.where(
            valid_now, jnp.where(section_pos == last_pos, skip_here, arriving_grad), 0.0
        )
        volume = take_slot(enc_inputs, slot_index).astype(jnp.float32)
        passed, cotangent_low, gain_part = backward_block(
            volume,
            enc_gain[0],
            enc_reverse,
            take_slot(enc_centre, slot_index),
            take_slot(enc_inverse, slot_index),
            incoming,
            counted,
        )
        enc_gain_sum = enc_gain_sum + gain_part
        enc_cotangents = store_slot(enc_cotangents, slot_index, valid_now, cotangent_low)
        leaving_grad = passed + skip_here
        if clock_step + 1 < clock_len:
            arriving_grad = passed_along(leaving_grad.astype(jnp.bfloat16), "section", -1).astype(
                leaving_grad.dtype
            )
    enc_gradient = weight_gradient(enc_grown, enc_cotangents)
    weight_all, gain_all = (
        lax.psum_scatter(
            jnp.stack([enc_gradient, dec_gradient]), ("rows", "dp"), scatter_dimension=1, tiled=True
        ),
        lax.psum_scatter(
            jnp.stack([enc_gain_sum, dec_gain_sum]), ("rows", "dp"), scatter_dimension=1, tiled=True
        ),
    )
    enc_result = weight_all[0:1]
    dec_result = weight_all[1:2]
    enc_gains = gain_all[0:1]
    dec_gains = gain_all[1:2]
    return (enc_result, dec_result, enc_gains, dec_gains)

MESH = pl.DeviceIdType.MESH
F32, BF16 = jnp.float32, jnp.bfloat16


def level_kernel(
    dims, counted, loss_scale, blocks,
    lat, grad, we_hbm, wd_hbm, ge, gd, group_ref,
    out_we, out_wd, out_ge, out_gd,
    we, wd, we_rev, wd_rev, patch, lat_cells, grad_cells,
    hin, din, ein, fin, hout, dout, eout, fout, yin,
    xhat_e, xhat_d, slope_e, slope_d, ga_s, skip, rstd_e, rstd_d,
    acts_e, acts_d, cots_e, cots_d, gains, vt_e, vt_d, gradient,
    w_sem, hop_send, hop_recv, half_send, half_recv, all_send, all_recv,
):
    ns, nr, nd = dims
    channels = ge.shape[1]
    per_row = 16
    cells = hin.shape[0]
    half = cells // 2
    s, r, d = (lax.axis_index(a) for a in ("section", "rows", "dp"))
    last = ns - 1
    peers = nr * nd
    me = r * nd + d

    def peer_id(k):
        p = lax.rem(me + k, peers)
        return (s, lax.div(p, nd), lax.rem(p, nd))

    def weight_copies(which):
        hbm, buf = ((we_hbm, we), (wd_hbm, wd))[which]
        span = 3 * channels
        return [
            pltpu.make_async_copy(
                hbm.at[dt, dh], buf.at[dh, pl.ds(dt * span, span)], w_sem.at[which, dt * 3 + dh]
            )
            for dt in range(3)
            for dh in range(3)
        ]

    for which in range(2):
        for c in weight_copies(which):
            c.start()

    barrier = pltpu.get_barrier_semaphore()
    for k in range(1, peers):
        pl.semaphore_signal(barrier, inc=1, device_id=peer_id(k), device_id_type=MESH)

    @pl.when(s > 0)
    def _():
        pl.semaphore_signal(barrier, inc=1, device_id=(s - 1, r, d), device_id_type=MESH)

    @pl.when(s < last)
    def _():
        pl.semaphore_signal(barrier, inc=1, device_id=(s + 1, r, d), device_id_type=MESH)

    def by_rows(ref):
        x = ref[...].astype(F32)
        x = jnp.stack([x[:, 0], x[:, 1]], axis=2)
        return x.reshape(2, half, channels).astype(BF16)

    patch[0:per_row, :] = jnp.zeros((per_row, patch.shape[1]), BF16)
    patch[cells + per_row :, :] = jnp.zeros((per_row, patch.shape[1]), BF16)

    lat_cells[...] = by_rows(lat)
    grad_cells[...] = by_rows(grad)
    pl.semaphore_wait(barrier, peers - 1 + (s > 0).astype(jnp.int32) + (s < last).astype(jnp.int32))

    def half_copy(i):
        source, target = ((lat_cells, hin), (grad_cells, yin))[i]
        return pltpu.make_async_remote_copy(
            src_ref=source.at[1 - r],
            dst_ref=target.at[pl.ds(pl.multiple_of(r * half, half), half)],
            send_sem=half_send.at[i],
            recv_sem=half_recv.at[i],
            device_id=(s, 1 - r, d),
            device_id_type=MESH,
        )

    @pl.when(s == 0)
    def _():
        half_copy(0).start()
        half_copy(1).start()
        mine = pl.ds(pl.multiple_of(r * half, half), half)
        hin[mine, :] = lat_cells[r]
        yin[mine, :] = grad_cells[r]
        half_copy(0).wait()

    def hop(i, step):
        source, target = ((hout, hin), (dout, din), (eout, ein), (fout, fin))[i]
        return pltpu.make_async_remote_copy(
            src_ref=source,
            dst_ref=target,
            send_sem=hop_send.at[i],
            recv_sem=hop_recv.at[i],
            device_id=(lax.rem(s + step + ns, ns), r, d),
            device_id_type=MESH,
        )

    def spread_copy(kind, k, owner):
        buf = (acts_e, acts_d, cots_d, cots_e, gains)[kind]
        return pltpu.make_async_remote_copy(
            src_ref=buf.at[me],
            dst_ref=buf.at[owner],
            send_sem=all_send.at[kind, k],
            recv_sem=all_recv.at[kind, k],
            device_id=peer_id(k),
            device_id_type=MESH,
        )

    def spread_start(kind):
        for k in range(1, peers):
            spread_copy(kind, k, me).start()

    def spread_wait(kind):
        for k in range(1, peers):
            c = spread_copy(kind, k, lax.rem(me - k + peers, peers))
            c.wait_send()
            c.wait_recv()

    row_at = lax.broadcasted_iota(jnp.int32, (16, channels), 0)

    def group_sums(vectors):
        stacked = jnp.zeros((16, channels), F32)
        at = 0
        for x in vectors:
            hi = x.astype(BF16).astype(F32)
            mid = (x - hi).astype(BF16).astype(F32)
            for part in (hi, mid, x - hi - mid):
                stacked = jnp.where(row_at == at, part, stacked)
                at += 1
        out = jnp.dot(stacked.astype(BF16), group_ref[...], preferred_element_type=F32)
        return [out[3 * i : 3 * i + 1] + out[3 * i + 1 : 3 * i + 2] + out[3 * i + 2 : 3 * i + 3]
                for i in range(len(vectors))]

    def cell_sum(x):
        return jnp.sum(x, axis=0, keepdims=True)

    col_at = lax.broadcasted_iota(jnp.int32, (cells // 8, 8, channels), 1)

    def conv(field, w_ref):
        v = field.reshape(cells // 8, 8, channels)
        zero = jnp.zeros_like(v)
        shifted = (
            jnp.where(col_at >= 1, pltpu.roll(v, 1, 1), zero),
            v,
            jnp.where(col_at <= 6, pltpu.roll(v, 7, 1), zero),
        )
        none = jnp.zeros((cells // 16, 1, 8, channels), F32)
        pieces = []
        for dt in range(3):
            for x in shifted:
                x = x.reshape(cells // 16, 2, 8, channels)
                if dt == 0:
                    x = jnp.concatenate([none, x[:, :1]], axis=1)
                elif dt == 2:
                    x = jnp.concatenate([x[:, 1:], none], axis=1)
                pieces.append(x.reshape(cells, channels).astype(BF16))
        patch[per_row : per_row + cells, :] = jnp.concatenate(pieces, axis=1)
        total = jnp.zeros((cells, channels), F32)
        for dh in range(3):
            total = total + jnp.dot(
                patch[dh * per_row : dh * per_row + cells, :], w_ref[dh],
                preferred_element_type=F32,
            )
        return total

    def normed(x, gain, xhat_ref, rstd_ref, acts):
        (mean,) = group_sums([cell_sum(x)])
        x = x - mean / counted
        (spread,) = group_sums([cell_sum(x * x)])
        inverse = lax.rsqrt(spread / counted + EPSILON)
        xhat = x * inverse
        z = xhat * gain
        a = (z * jax.nn.sigmoid(z)).astype(BF16)
        xhat_ref[...] = xhat
        rstd_ref[...] = inverse
        acts[me] = a
        return a.astype(F32)

    def slope(xhat_ref, gain, slope_ref):
        z = xhat_ref[...] * gain
        sg = jax.nn.sigmoid(z)
        slope_ref[...] = sg * (1.0 + z * (1.0 - sg))

    def reverse_weights():
        for source, target in ((wd, wd_rev), (we, we_rev)):
            def turn(j, _, source=source, target=target):
                dh = lax.div(j, 9)
                b = lax.rem(j, 9)
                block = source[dh, pl.ds(pl.multiple_of(b * channels, channels), channels), :]
                target[2 - dh, pl.ds(pl.multiple_of((8 - b) * channels, channels), channels), :] = (
                    block.astype(F32).T.astype(BF16)
                )
                return 0
            lax.fori_loop(0, 27, turn, 0)

    share = out_we.shape[1]
    first_block = lax.div(me * share, channels)

    def shifted_acts(kind):
        buf, target = ((acts_e, vt_e), (acts_d, vt_d))[kind]
        cell = lax.broadcasted_iota(jnp.int32, (cells, channels), 0)
        row, frame, col = cell >> 4, (cell >> 3) & 1, cell & 7
        rows_all = cells // 16

        for j in range(blocks):
            b = jnp.minimum(first_block + j, 26)
            dt, dh, dw = lax.div(b, 9) - 1, lax.rem(lax.div(b, 3), 3) - 1, lax.rem(b, 3) - 1
            turn = lax.rem(cells - (dh * 16 + dt * 8 + dw), cells)
            valid = (
                (row + dh >= 0) & (row + dh < rows_all)
                & (frame + dt >= 0) & (frame + dt < 2)
                & (col + dw >= 0) & (col + dw < 8)
            )

            def one(p, _, j=j, turn=turn, valid=valid):
                x = pltpu.roll(buf[p].astype(F32), turn, 0)
                x = jnp.where(valid, x, 0.0).T.astype(BF16)
                target[j, :, pl.ds(pl.multiple_of(p * cells, cells), cells)] = x
                return 0

            lax.fori_loop(0, peers, one, 0)

    def weight_grads(kind):
        cots, vt, out = ((cots_e, vt_e, out_we), (cots_d, vt_d, out_wd))[kind]
        flat = cots[...].reshape(peers * cells, channels)
        for j in range(blocks):
            gradient[j * channels : (j + 1) * channels, :] = jnp.dot(
                vt[j], flat, preferred_element_type=F32
            )
        begin = pl.multiple_of(me * share - first_block * channels, 8)
        out[0] = gradient[pl.ds(begin, share), :]

    def backward(ga, y, gain, xhat_ref, slope_ref, rstd_ref):
        gz = ga * slope_ref[...]
        xhat = xhat_ref[...]
        gx = gz * gain
        first, second = group_sums([cell_sum(gx), cell_sum(gx * xhat)])
        result = y + rstd_ref[...] * (gx - first / counted - xhat * (second / counted))
        return result, gz * xhat

    @pl.when(s > 0)
    def _():
        hop(0, -1).wait_recv()

    for c in weight_copies(0):
        c.wait()
    x = hin[...].astype(F32)
    result = x + conv(normed(x, ge[...], xhat_e, rstd_e, acts_e), we)
    h = result.astype(BF16)

    @pl.when(s < last)
    def _():
        hout[...] = h
        hop(0, 1).start()

    @pl.when(s == last)
    def _():
        din[...] = h

    spread_start(0)
    for c in weight_copies(1):
        c.wait()

    def first_idle():
        slope(xhat_e, ge[...], slope_e)
        reverse_weights()

    @pl.when(s < last)
    def _():
        first_idle()

        @pl.when(s == 0)
        def _():
            half_copy(1).wait()
            y = yin[...].astype(F32) * loss_scale
            yb = y.astype(BF16)
            cots_d[me] = yb
            ga_s[...] = conv(yb.astype(F32), wd_rev)
            spread_start(2)

        spread_wait(0)
        shifted_acts(0)
        hop(0, 1).wait_send()
        hop(1, 1).wait_recv()

    u = din[...].astype(F32) + hin[...].astype(F32)
    a = normed(u, gd[...], xhat_d, rstd_d, acts_d)

    @pl.when(s > 0)
    def _():
        dout[...] = (u + conv(a, wd)).astype(BF16)
        hop(1, -1).start()

    slope(xhat_d, gd[...], slope_d)

    @pl.when(s == last)
    def _():
        spread_start(1)
        first_idle()
        spread_wait(0)
        shifted_acts(0)
        spread_wait(1)
        shifted_acts(1)

    @pl.when(s > 0)
    def _():
        hop(2, -1).wait_recv()
        yb = ein[...]
        cots_d[me] = yb
        ga_s[...] = conv(yb.astype(F32), wd_rev)
        yin[...] = yb

    y = jnp.where(s == 0, loss_scale, 1.0) * yin[...].astype(F32)
    c, gain_cells = backward(ga_s[...], y, gd[...], xhat_d, slope_d, rstd_d)
    skip[...] = c

    @pl.when(s < last)
    def _():
        eout[...] = c.astype(BF16)
        hop(2, 1).start()
        spread_start(1)

    dec_gain_row = cell_sum(gain_cells)

    @pl.when(s > 0)
    def _():
        spread_start(2)

    @pl.when(s < last)
    def _():
        spread_wait(1)
        shifted_acts(1)
        spread_wait(2)
        weight_grads(1)
        hop(2, 1).wait_send()
        hop(3, 1).wait_recv()

    c = skip[...]
    y = jnp.where(s == last, c, fin[...].astype(F32))
    yb = y.astype(BF16)
    cots_e[me] = yb
    spread_start(3)
    ga = conv(yb.astype(F32), we_rev)
    f, gain_cells = backward(ga, y, ge[...], xhat_e, slope_e, rstd_e)

    @pl.when(s > 0)
    def _():
        fout[...] = (f + c).astype(BF16)
        hop(3, -1).start()

    enc_gain_row = cell_sum(gain_cells)
    at8 = lax.broadcasted_iota(jnp.int32, (8, channels), 0)
    gains[me] = jnp.where(at8 == 0, enc_gain_row, jnp.where(at8 == 1, dec_gain_row, 0.0))
    spread_start(4)

    @pl.when(s == last)
    def _():
        spread_wait(2)
        weight_grads(1)

    spread_wait(3)
    weight_grads(0)
    spread_wait(4)
    total = jnp.sum(gains[...], axis=0)
    width = out_ge.shape[1]
    piece = total[:, 0:width]
    for i in range(1, peers):
        piece = jnp.where(me == i, total[:, i * width : (i + 1) * width], piece)
    out_ge[...] = piece[0:1]
    out_gd[...] = piece[1:2]

    @pl.when(s > 0)
    def _():
        hop(1, -1).wait_send()
        hop(3, -1).wait_send()


def one_kernel(latent, enc_weight, dec_weight, enc_gain, dec_gain, out_grad):
    batches, frames, rows_here, columns, channels = latent.shape
    ns, nr, nd = (lax.axis_size(a) for a in ("section", "rows", "dp"))
    peers = nr * nd
    cells = frames * rows_here * nr * columns
    counted = cells * (channels // GROUPS)
    loss_scale = 1.0 / math.sqrt(batches * nd * cells)
    taps = 27 * channels
    share = taps // peers
    blocks = max(
        min((i * share + share - 1) // channels, 26) - i * share // channels + 1
        for i in range(peers)
    )
    owner = np.arange(channels) // (channels // GROUPS)
    groups = jnp.asarray(owner[:, None] == owner[None, :], BF16)
    field = pltpu.VMEM((cells, channels), BF16)
    wide = pltpu.VMEM((cells, channels), F32)
    weights = pltpu.VMEM((3, 9 * channels, channels), BF16)
    every = pltpu.VMEM((peers, cells, channels), BF16)
    vector = pltpu.VMEM((1, channels), F32)
    vmem = pl.BlockSpec(memory_space=pltpu.VMEM)
    anywhere = pl.BlockSpec(memory_space=pl.ANY)
    dma = pltpu.SemaphoreType.DMA
    split = (3, 3, 3 * channels, channels)
    flops = 2 * cells * taps * channels * 4 + 4 * share * peers * cells * channels
    return pl.pallas_call(
        functools.partial(level_kernel, (ns, nr, nd), float(counted), loss_scale, blocks),
        out_shape=(
            jax.ShapeDtypeStruct((1, share, channels), F32),
            jax.ShapeDtypeStruct((1, share, channels), F32),
            jax.ShapeDtypeStruct((1, channels // peers), F32),
            jax.ShapeDtypeStruct((1, channels // peers), F32),
        ),
        in_specs=[vmem, vmem, anywhere, anywhere, vmem, vmem, vmem],
        out_specs=(vmem, vmem, vmem, vmem),
        scratch_shapes=[
            weights, weights, weights, weights,
            pltpu.VMEM((cells + 32, 9 * channels), BF16),
            pltpu.VMEM((2, cells // 2, channels), BF16),
            pltpu.VMEM((2, cells // 2, channels), BF16),
            field, field, field, field, field, field, field, field, field,
            wide, wide, wide, wide, wide, wide, vector, vector,
            every, every, every, every,
            pltpu.VMEM((peers, 8, channels), F32),
            pltpu.VMEM((blocks, channels, peers * cells), BF16),
            pltpu.VMEM((blocks, channels, peers * cells), BF16),
            pltpu.VMEM((blocks * channels, channels), F32),
            dma((2, 9)), dma((4,)), dma((4,)), dma((2,)), dma((2,)),
            dma((5, peers)), dma((5, peers)),
        ],
        compiler_params=pltpu.CompilerParams(
            collective_id=0, has_side_effects=True, vmem_limit_bytes=48 * 1024 * 1024
        ),
        cost_estimate=pl.CostEstimate(
            flops=flops, bytes_accessed=4 * taps * channels, transcendentals=4 * cells * channels
        ),
    )(
        latent, out_grad, enc_weight.reshape(split), dec_weight.reshape(split),
        enc_gain, dec_gain, groups,
    )


def per_device(latent, *rest):
    batches, frames, rows_here, columns, channels = latent.shape
    rows, dp = lax.axis_size("rows"), lax.axis_size("dp")
    taps = 27 * channels
    fits = (
        rows == 2 and batches == 2 and frames == 2 and columns == 8 and rows_here % 4 == 0
        and rows_here * rows * 16 == 128
        and taps % (8 * rows * dp) == 0 and channels % 64 == 0 and channels % (rows * dp) == 0
        and lax.axis_size("section") > 1
    )
    return (one_kernel if fits else on_device)(latent, *rest)


def solution(mesh):
    in_specs = (
        P("dp", None, "rows", None, None),
        P("section", None, None),
        P("section", None, None),
        P("section", None),
        P("section", None),
        P("dp", None, "rows", None, None),
    )
    out_specs = (
        P("section", ("rows", "dp"), None),
        P("section", ("rows", "dp"), None),
        P("section", ("rows", "dp")),
        P("section", ("rows", "dp")),
    )
    return jax.shard_map(
        per_device, mesh=mesh, in_specs=in_specs, out_specs=out_specs, check_vma=False
    )
```

```python
import functools
import math

import jax
import jax.numpy as jnp
import numpy as np
from jax import lax
from jax.experimental import pallas as pl
from jax.experimental.pallas import tpu as pltpu
from jax.sharding import PartitionSpec as P

GROUPS = 32


EPSILON = 1e-05


def padded_2(block, sides, width):
    for axis, dim in sides:
        count = lax.axis_size(axis)
        forward = [(i, i + 1) for i in range(count - 1)]
        backward = [(target, source) for source, target in forward]
        low = lax.ppermute(
            lax.slice_in_dim(block, block.shape[dim] - width, None, axis=dim), axis, forward
        )
        high = lax.ppermute(lax.slice_in_dim(block, 0, width, axis=dim), axis, backward)
        block = jnp.concatenate([low, block, high], axis=dim)
    return block


def passed_along(block, axis, distance):
    devices = range(lax.axis_size(axis))
    route = [(i - distance, i) for i in devices if i - distance in devices]
    return lax.ppermute(block, axis, route)


def spread_groups(values, channels):
    return jnp.repeat(values, channels // GROUPS)


def gather_patches(grown_rows):
    frames, padded_rows, columns, channels = grown_rows.shape
    inner_rows = padded_rows - 2
    padded = jnp.pad(grown_rows, ((1, 1), (0, 0), (1, 1), (0, 0)))
    pieces = []
    for lag_frame in range(3):
        for lag_row in range(3):
            for lag_column in range(3):
                pieces.append(
                    padded[
                        lag_frame : lag_frame + frames,
                        lag_row : lag_row + inner_rows,
                        lag_column : lag_column + columns,
                        :,
                    ]
                )
    return jnp.concatenate(pieces, axis=-1).reshape(frames * inner_rows * columns, 27 * channels)


def flipped(weights):
    channels = weights.shape[1]
    blocks = weights.reshape(27, -1, channels)[::-1]
    return jnp.swapaxes(blocks, 1, 2).reshape(-1, blocks.shape[1])


def take_slot(buffer, slot_index):
    return lax.dynamic_index_in_dim(buffer, slot_index, 0, keepdims=False)


def store_slot(buffer, slot_index, valid_now, new_value):
    kept = jnp.where(valid_now, new_value, take_slot(buffer, slot_index))
    return lax.dynamic_update_index_in_dim(buffer, kept, slot_index, 0)


def weight_gradient(grown_all, cotangent_all):
    patches = jax.vmap(gather_patches)(grown_all)
    patches = patches.reshape(-1, patches.shape[-1])
    flat_cot = cotangent_all.reshape(-1, cotangent_all.shape[-1])
    return lax.dot_general(
        patches, flat_cot, (((0,), (0,)), ((), ())), preferred_element_type=jnp.float32
    )


def norm_stats(volume, counted):
    grouped = volume.reshape(-1, GROUPS, volume.shape[-1] // GROUPS)
    totals = lax.psum(jnp.sum(grouped, axis=(0, 2)), "rows")
    centre = totals / counted
    deviation = grouped - centre[None, :, None]
    spread = lax.psum(jnp.sum(deviation * deviation, axis=(0, 2)), "rows") / counted
    return (centre, lax.rsqrt(spread + EPSILON))


def forward_block(volume, gain_vec, weights, counted):
    channels = volume.shape[-1]
    centre, inverse = norm_stats(volume, counted)
    normed = (volume - spread_groups(centre, channels)) * spread_groups(inverse, channels)
    active = jax.nn.silu(normed * gain_vec).astype(jnp.bfloat16)
    grown_act = padded_2(active, (("rows", 1),), 1)
    conv_out = jnp.dot(gather_patches(grown_act), weights, preferred_element_type=jnp.float32)
    return (grown_act, centre, inverse, volume + conv_out.reshape(volume.shape))


def backward_block(volume, gain_vec, reverse_weights, centre, inverse, cotangent, counted):
    channels = volume.shape[-1]
    inverse_full = spread_groups(inverse, channels)
    normed = (volume - spread_groups(centre, channels)) * inverse_full
    zvalue = normed * gain_vec
    cotangent_low = cotangent.astype(jnp.bfloat16)
    grown_cot = padded_2(cotangent_low, (("rows", 1),), 1)
    act_grad = jnp.dot(
        gather_patches(grown_cot), reverse_weights, preferred_element_type=jnp.float32
    ).reshape(volume.shape)
    logistic = jax.nn.sigmoid(zvalue)
    pre_grad = act_grad * logistic * (1.0 + zvalue * (1.0 - logistic))
    hat_grad = pre_grad * gain_vec
    grouped_grad = hat_grad.reshape(-1, GROUPS, channels // GROUPS)
    grouped_hat = normed.reshape(-1, GROUPS, channels // GROUPS)
    first_sum, second_sum = lax.psum(
        (jnp.sum(grouped_grad, axis=(0, 2)), jnp.sum(grouped_grad * grouped_hat, axis=(0, 2))),
        "rows",
    )
    input_grad = inverse_full * (
        hat_grad
        - spread_groups(first_sum / counted, channels)
        - normed * spread_groups(second_sum / counted, channels)
    )
    gain_part = jnp.sum((pre_grad * normed).reshape(-1, channels), axis=0)
    return (cotangent + input_grad, cotangent_low, gain_part)


def on_device(latent, enc_weight, dec_weight, enc_gain, dec_gain, out_grad):
    section_pos = lax.axis_index("section")
    section_count = lax.axis_size("section")
    batches, frames, rows_here, columns, channels = latent.shape
    counted = frames * rows_here * columns * (channels // GROUPS) * lax.axis_size("rows")
    cells_all = batches * lax.axis_size("dp") * frames * rows_here * lax.axis_size("rows") * columns
    loss_scale = 1.0 / math.sqrt(cells_all)
    clock_len = batches + section_count - 1
    last_pos = section_count - 1
    grown_shape = (batches, frames, rows_here + 2, columns, channels)
    enc_inputs = jnp.zeros(latent.shape, jnp.bfloat16)
    enc_tops = jnp.zeros(latent.shape, jnp.bfloat16)
    enc_grown = jnp.zeros(grown_shape, jnp.bfloat16)
    enc_centre = jnp.zeros((batches, GROUPS), jnp.float32)
    enc_inverse = jnp.zeros((batches, GROUPS), jnp.float32)
    arriving = jnp.zeros(latent.shape[1:], jnp.bfloat16)
    for clock_step in range(clock_len):
        micro_index = clock_step - section_pos
        valid_now = (micro_index >= 0) & (micro_index < batches)
        slot_index = jnp.clip(micro_index, 0, batches - 1)
        entering = jnp.where(section_pos == 0, latent[min(clock_step, batches - 1)], arriving)
        grown_act, centre, inverse, result = forward_block(
            entering.astype(jnp.float32), enc_gain[0], enc_weight[0], counted
        )
        leaving = result.astype(jnp.bfloat16)
        enc_inputs = store_slot(enc_inputs, slot_index, valid_now, entering)
        enc_tops = store_slot(enc_tops, slot_index, valid_now, leaving)
        enc_grown = store_slot(enc_grown, slot_index, valid_now, grown_act)
        enc_centre = store_slot(enc_centre, slot_index, valid_now, centre)
        enc_inverse = store_slot(enc_inverse, slot_index, valid_now, inverse)
        if clock_step + 1 < clock_len:
            arriving = passed_along(leaving, "section", 1)
    dec_downs = jnp.zeros(latent.shape, jnp.bfloat16)
    dec_grown = jnp.zeros(grown_shape, jnp.bfloat16)
    dec_centre = jnp.zeros((batches, GROUPS), jnp.float32)
    dec_inverse = jnp.zeros((batches, GROUPS), jnp.float32)
    arriving = jnp.zeros(latent.shape[1:], jnp.bfloat16)
    for clock_step in range(clock_len):
        micro_index = clock_step - (last_pos - section_pos)
        valid_now = (micro_index >= 0) & (micro_index < batches)
        slot_index = jnp.clip(micro_index, 0, batches - 1)
        coming = jnp.where(section_pos == last_pos, take_slot(enc_tops, slot_index), arriving)
        united = coming.astype(jnp.float32) + take_slot(enc_inputs, slot_index).astype(jnp.float32)
        grown_act, centre, inverse, result = forward_block(
            united, dec_gain[0], dec_weight[0], counted
        )
        dec_downs = store_slot(dec_downs, slot_index, valid_now, coming)
        dec_grown = store_slot(dec_grown, slot_index, valid_now, grown_act)
        dec_centre = store_slot(dec_centre, slot_index, valid_now, centre)
        dec_inverse = store_slot(dec_inverse, slot_index, valid_now, inverse)
        if clock_step + 1 < clock_len:
            arriving = passed_along(result.astype(jnp.bfloat16), "section", -1)
    dec_reverse = flipped(dec_weight[0])
    skip_grads = jnp.zeros(latent.shape, jnp.float32)
    dec_cotangents = jnp.zeros(latent.shape, jnp.bfloat16)
    dec_gain_sum = jnp.zeros((channels,), jnp.float32)
    arriving_grad = jnp.zeros(latent.shape[1:], jnp.float32)
    for clock_step in range(clock_len):
        micro_index = clock_step - section_pos
        valid_now = (micro_index >= 0) & (micro_index < batches)
        slot_index = jnp.clip(micro_index, 0, batches - 1)
        seeded = out_grad[min(clock_step, batches - 1)].astype(jnp.float32) * loss_scale
        incoming = jnp.where(valid_now, jnp.where(section_pos == 0, seeded, arriving_grad), 0.0)
        united = take_slot(dec_downs, slot_index).astype(jnp.float32) + take_slot(
            enc_inputs, slot_index
        ).astype(jnp.float32)
        passed, cotangent_low, gain_part = backward_block(
            united,
            dec_gain[0],
            dec_reverse,
            take_slot(dec_centre, slot_index),
            take_slot(dec_inverse, slot_index),
            incoming,
            counted,
        )
        dec_gain_sum = dec_gain_sum + gain_part
        dec_cotangents = store_slot(dec_cotangents, slot_index, valid_now, cotangent_low)
        skip_grads = store_slot(skip_grads, slot_index, valid_now, passed)
        if clock_step + 1 < clock_len:
            arriving_grad = passed_along(passed.astype(jnp.bfloat16), "section", 1).astype(
                passed.dtype
            )
    dec_gradient = weight_gradient(dec_grown, dec_cotangents)
    enc_reverse = flipped(enc_weight[0])
    enc_cotangents = jnp.zeros(latent.shape, jnp.bfloat16)
    enc_gain_sum = jnp.zeros((channels,), jnp.float32)
    arriving_grad = jnp.zeros(latent.shape[1:], jnp.float32)
    for clock_step in range(clock_len):
        micro_index = clock_step - (last_pos - section_pos)
        valid_now = (micro_index >= 0) & (micro_index < batches)
        slot_index = jnp.clip(micro_index, 0, batches - 1)
        skip_here = take_slot(skip_grads, slot_index)
        incoming = jnp.where(
            valid_now, jnp.where(section_pos == last_pos, skip_here, arriving_grad), 0.0
        )
        volume = take_slot(enc_inputs, slot_index).astype(jnp.float32)
        passed, cotangent_low, gain_part = backward_block(
            volume,
            enc_gain[0],
            enc_reverse,
            take_slot(enc_centre, slot_index),
            take_slot(enc_inverse, slot_index),
            incoming,
            counted,
        )
        enc_gain_sum = enc_gain_sum + gain_part
        enc_cotangents = store_slot(enc_cotangents, slot_index, valid_now, cotangent_low)
        leaving_grad = passed + skip_here
        if clock_step + 1 < clock_len:
            arriving_grad = passed_along(leaving_grad.astype(jnp.bfloat16), "section", -1).astype(
                leaving_grad.dtype
            )
    enc_gradient = weight_gradient(enc_grown, enc_cotangents)
    weight_all, gain_all = (
        lax.psum_scatter(
            jnp.stack([enc_gradient, dec_gradient]), ("rows", "dp"), scatter_dimension=1, tiled=True
        ),
        lax.psum_scatter(
            jnp.stack([enc_gain_sum, dec_gain_sum]), ("rows", "dp"), scatter_dimension=1, tiled=True
        ),
    )
    enc_result = weight_all[0:1]
    dec_result = weight_all[1:2]
    enc_gains = gain_all[0:1]
    dec_gains = gain_all[1:2]
    return (enc_result, dec_result, enc_gains, dec_gains)

MESH = pl.DeviceIdType.MESH
F32, BF16 = jnp.float32, jnp.bfloat16


def level_kernel(
    dims, counted, loss_scale, blocks,
    lat, grad, we_hbm, wd_hbm, ge, gd, group_ref,
    out_we, out_wd, out_ge, out_gd,
    wt_e, wt_d, we, wd, we_rev, wd_rev, lat_cells, grad_cells,
    hin, din, ein, fin, hout, dout, eout, fout, yin,
    xhat_e, xhat_d, slope_e, slope_d, ga_s, skip, rstd_e, rstd_d,
    acts_e, acts_d, cots_e, cots_d, gains, vt_e, vt_d, gradient,
    w_sem, hop_send, hop_recv, half_send, half_recv, all_send, all_recv,
):
    ns, nr, nd = dims
    channels = ge.shape[1]
    cells = hin.shape[0]
    half = cells // 2
    s, r, d = (lax.axis_index(a) for a in ("section", "rows", "dp"))
    last = ns - 1
    peers = nr * nd
    me = r * nd + d

    def peer_id(k):
        p = lax.rem(me + k, peers)
        return (s, lax.div(p, nd), lax.rem(p, nd))

    def weight_copy(which):
        hbm, buf = ((we_hbm, wt_e), (wd_hbm, wt_d))[which]
        return pltpu.make_async_copy(hbm.at[0], buf, w_sem.at[which])

    weight_copy(0).start()
    weight_copy(1).start()

    barrier = pltpu.get_barrier_semaphore()
    for k in range(1, peers):
        pl.semaphore_signal(barrier, inc=1, device_id=peer_id(k), device_id_type=MESH)

    @pl.when(s > 0)
    def _():
        pl.semaphore_signal(barrier, inc=1, device_id=(s - 1, r, d), device_id_type=MESH)

    @pl.when(s < last)
    def _():
        pl.semaphore_signal(barrier, inc=1, device_id=(s + 1, r, d), device_id_type=MESH)

    def by_rows(ref):
        x = ref[...].astype(F32)
        x = jnp.stack([x[:, 0], x[:, 1]], axis=2)
        return x.reshape(2, half, channels).astype(BF16)

    lat_cells[...] = by_rows(lat)
    grad_cells[...] = by_rows(grad)
    pl.semaphore_wait(barrier, peers - 1 + (s > 0).astype(jnp.int32) + (s < last).astype(jnp.int32))

    def half_copy(i):
        source, target = ((lat_cells, hin), (grad_cells, yin))[i]
        return pltpu.make_async_remote_copy(
            src_ref=source.at[1 - r],
            dst_ref=target.at[pl.ds(pl.multiple_of(r * half, half), half)],
            send_sem=half_send.at[i],
            recv_sem=half_recv.at[i],
            device_id=(s, 1 - r, d),
            device_id_type=MESH,
        )

    @pl.when(s == 0)
    def _():
        half_copy(0).start()
        half_copy(1).start()
        mine = pl.ds(pl.multiple_of(r * half, half), half)
        hin[mine, :] = lat_cells[r]
        yin[mine, :] = grad_cells[r]

    def hop(i, step):
        source, target = ((hout, hin), (dout, din), (eout, ein), (fout, fin))[i]
        return pltpu.make_async_remote_copy(
            src_ref=source,
            dst_ref=target,
            send_sem=hop_send.at[i],
            recv_sem=hop_recv.at[i],
            device_id=(lax.rem(s + step + ns, ns), r, d),
            device_id_type=MESH,
        )

    def spread_copy(kind, k, owner):
        buf = (acts_e, acts_d, cots_d, cots_e, gains)[kind]
        return pltpu.make_async_remote_copy(
            src_ref=buf.at[me],
            dst_ref=buf.at[owner],
            send_sem=all_send.at[kind, k],
            recv_sem=all_recv.at[kind, k],
            device_id=peer_id(k),
            device_id_type=MESH,
        )

    def spread_start(kind):
        for k in range(1, peers):
            spread_copy(kind, k, me).start()

    def spread_wait(kind):
        for k in range(1, peers):
            c = spread_copy(kind, k, lax.rem(me - k + peers, peers))
            c.wait_send()
            c.wait_recv()

    row_at = lax.broadcasted_iota(jnp.int32, (16, channels), 0)

    def group_sums(vectors):
        stacked = jnp.zeros((16, channels), F32)
        at = 0
        for x in vectors:
            hi = x.astype(BF16).astype(F32)
            mid = (x - hi).astype(BF16).astype(F32)
            for part in (hi, mid, x - hi - mid):
                stacked = jnp.where(row_at == at, part, stacked)
                at += 1
        out = jnp.dot(stacked.astype(BF16), group_ref[...], preferred_element_type=F32)
        return [out[3 * i : 3 * i + 1] + out[3 * i + 1 : 3 * i + 2] + out[3 * i + 2 : 3 * i + 3]
                for i in range(len(vectors))]

    def cell_sum(x):
        return jnp.sum(x, axis=0, keepdims=True)

    col_at = lax.broadcasted_iota(jnp.int32, (cells // 8, 8, channels), 1)

    def conv(field, w_ref):
        v = field.reshape(cells // 8, 8, channels)
        zero = jnp.zeros_like(v)
        shifted = (
            jnp.where(col_at >= 1, pltpu.roll(v, 1, 1), zero),
            v,
            jnp.where(col_at <= 6, pltpu.roll(v, 7, 1), zero),
        )
        none = jnp.zeros((cells // 16, 1, 8, channels), F32)
        edge = jnp.zeros((16, channels), BF16)
        pieces = []
        for dt in range(3):
            framed = []
            for x in shifted:
                x = x.reshape(cells // 16, 2, 8, channels)
                if dt == 0:
                    x = jnp.concatenate([none, x[:, :1]], axis=1)
                elif dt == 2:
                    x = jnp.concatenate([x[:, 1:], none], axis=1)
                framed.append(x.reshape(cells, channels).astype(BF16))
            pieces += [jnp.concatenate([edge, x[: cells - 16]], axis=0) for x in framed]
            pieces += framed
            pieces += [jnp.concatenate([x[16:], edge], axis=0) for x in framed]
        total = jnp.zeros((cells, channels), F32)
        for at in range(0, 27, 4):
            chunk = pieces[at : at + 4]
            total = total + jnp.dot(
                jnp.concatenate(chunk, axis=1),
                w_ref[at * channels : (at + len(chunk)) * channels, :],
                preferred_element_type=F32,
            )
        return total

    def normed(x, gain, xhat_ref, rstd_ref, acts):
        (mean,) = group_sums([cell_sum(x)])
        x = x - mean / counted
        (spread,) = group_sums([cell_sum(x * x)])
        inverse = lax.rsqrt(spread / counted + EPSILON)
        xhat = x * inverse
        z = xhat * gain
        a = (z * jax.nn.sigmoid(z)).astype(BF16)
        xhat_ref[...] = xhat
        rstd_ref[...] = inverse
        acts[me] = a
        return a.astype(F32)

    def slope(xhat_ref, gain, slope_ref):
        z = xhat_ref[...] * gain
        sg = jax.nn.sigmoid(z)
        slope_ref[...] = sg * (1.0 + z * (1.0 - sg))

    def turn_weights(source, target):
        step = 2 * channels
        whole = 27 * channels // step

        def turn(j, _):
            at = pl.ds(pl.multiple_of(j * step, step), step)
            target[at, :] = source[:, at].astype(F32).T.astype(BF16)
            return 0

        lax.fori_loop(0, whole, turn, 0)
        target[whole * step :, :] = source[:, whole * step :].astype(F32).T.astype(BF16)

    def reverse_weights(source, target):
        for o in range(27):
            target[(26 - o) * channels : (27 - o) * channels, :] = source[
                :, o * channels : (o + 1) * channels
            ]

    share = 27 * channels // peers
    first_block = lax.div(me * share, channels)

    def shifted_acts(kind):
        buf, target = ((acts_e, vt_e), (acts_d, vt_d))[kind]
        cell = lax.broadcasted_iota(jnp.int32, (cells, channels), 0)
        row, frame, col = cell >> 4, (cell >> 3) & 1, cell & 7
        rows_all = cells // 16

        for j in range(blocks):
            b = jnp.minimum(first_block + j, 26)
            dt, dh, dw = lax.div(b, 9) - 1, lax.rem(lax.div(b, 3), 3) - 1, lax.rem(b, 3) - 1
            turn = lax.rem(cells - (dh * 16 + dt * 8 + dw), cells)
            valid = (
                (row + dh >= 0) & (row + dh < rows_all)
                & (frame + dt >= 0) & (frame + dt < 2)
                & (col + dw >= 0) & (col + dw < 8)
            )

            def one(p, _, j=j, turn=turn, valid=valid):
                x = pltpu.roll(buf[p].astype(F32), turn, 0)
                x = jnp.where(valid, x, 0.0).T.astype(BF16)
                target[j, :, pl.ds(pl.multiple_of(p * cells, cells), cells)] = x
                return 0

            lax.fori_loop(0, peers, one, 0)

    def weight_grads(kind):
        cots, vt, out = ((cots_e, vt_e, out_we), (cots_d, vt_d, out_wd))[kind]
        flat = cots[...].reshape(peers * cells, channels)
        for j in range(blocks):
            gradient[j * channels : (j + 1) * channels, :] = jnp.dot(
                vt[j], flat, preferred_element_type=F32
            )
        begin = pl.multiple_of(me * share - first_block * channels, 8)
        out[0] = gradient[pl.ds(begin, share), :].T

    def backward(ga, y, gain, xhat_ref, slope_ref, rstd_ref):
        gz = ga * slope_ref[...]
        xhat = xhat_ref[...]
        gx = gz * gain
        first, second = group_sums([cell_sum(gx), cell_sum(gx * xhat)])
        result = y + rstd_ref[...] * (gx - first / counted - xhat * (second / counted))
        return result, gz * xhat

    def near_copy(j, owner):
        if j == 0:
            to = (s, 1 - r, d)
        else:
            to = (s, r, lax.rem(d + j, nd))
        return pltpu.make_async_remote_copy(
            src_ref=cots_e.at[me],
            dst_ref=cots_e.at[owner],
            send_sem=all_send.at[3, j],
            recv_sem=all_recv.at[3, j],
            device_id=to,
            device_id_type=MESH,
        )

    def relay_copy(j, core):
        owner = core * nd + lax.rem(d - j + nd, nd)
        return pltpu.make_async_remote_copy(
            src_ref=cots_e.at[owner],
            dst_ref=cots_e.at[owner],
            send_sem=all_send.at[3, nd - 1 + j],
            recv_sem=all_recv.at[3, nd - 1 + j],
            device_id=(s, 1 - r, d),
            device_id_type=MESH,
        )

    late = 2 * s >= ns

    weight_copy(0).wait()
    turn_weights(wt_e, we)

    @pl.when(s > 0)
    def _():
        weight_copy(1).wait()
        turn_weights(wt_d, wd)
        hop(0, -1).wait_recv()

    @pl.when(s == 0)
    def _():
        half_copy(0).wait()

    x = hin[...].astype(F32)
    result = x + conv(normed(x, ge[...], xhat_e, rstd_e, acts_e), we)
    h = result.astype(BF16)

    @pl.when(s < last)
    def _():
        hout[...] = h
        hop(0, 1).start()

    @pl.when(s == last)
    def _():
        din[...] = h

    spread_start(0)

    @pl.when(s == 0)
    def _():
        weight_copy(1).wait()

    def first_idle():
        slope(xhat_e, ge[...], slope_e)
        reverse_weights(wt_d, wd_rev)
        reverse_weights(wt_e, we_rev)

        @pl.when(s == 0)
        def _():
            half_copy(1).wait()
            y = yin[...].astype(F32) * loss_scale
            yb = y.astype(BF16)
            cots_d[me] = yb
            ga_s[...] = conv(yb.astype(F32), wd_rev)
            spread_start(2)

        spread_wait(0)
        shifted_acts(0)

    @pl.when(jnp.logical_not(late))
    def _():
        first_idle()

    @pl.when(s < last)
    def _():
        hop(0, 1).wait_send()
        hop(1, 1).wait_recv()

    u = din[...].astype(F32) + hin[...].astype(F32)
    a = normed(u, gd[...], xhat_d, rstd_d, acts_d)

    @pl.when(s > 0)
    def _():
        dout[...] = (u + conv(a, wd)).astype(BF16)
        hop(1, -1).start()
        spread_start(1)

    slope(xhat_d, gd[...], slope_d)

    @pl.when(late)
    def _():
        first_idle()
        spread_wait(1)
        shifted_acts(1)

    @pl.when(s > 0)
    def _():
        hop(2, -1).wait_recv()
        yb = ein[...]
        cots_d[me] = yb
        ga_s[...] = conv(yb.astype(F32), wd_rev)
        yin[...] = yb

    y = jnp.where(s == 0, loss_scale, 1.0) * yin[...].astype(F32)
    c, gain_cells = backward(ga_s[...], y, gd[...], xhat_d, slope_d, rstd_d)
    skip[...] = c

    @pl.when(s < last)
    def _():
        eout[...] = c.astype(BF16)
        hop(2, 1).start()

    dec_gain_row = cell_sum(gain_cells)

    @pl.when(s == 0)
    def _():
        spread_start(1)

    @pl.when(s > 0)
    def _():
        spread_start(2)

    @pl.when(jnp.logical_not(late))
    def _():
        spread_wait(1)
        shifted_acts(1)
        spread_wait(2)
        weight_grads(1)

    @pl.when(s < last)
    def _():
        hop(2, 1).wait_send()
        hop(3, 1).wait_recv()

    c = skip[...]
    y = jnp.where(s == last, c, fin[...].astype(F32))
    yb = y.astype(BF16)
    cots_e[me] = yb
    for j in range(nd - 1, -1, -1):
        near_copy(j, me).start()
    ga = conv(yb.astype(F32), we_rev)
    f, gain_cells = backward(ga, y, ge[...], xhat_e, slope_e, rstd_e)

    @pl.when(s > 0)
    def _():
        fout[...] = (f + c).astype(BF16)
        hop(3, -1).start()

    enc_gain_row = cell_sum(gain_cells)
    at8 = lax.broadcasted_iota(jnp.int32, (8, channels), 0)
    gains[me] = jnp.where(at8 == 0, enc_gain_row, jnp.where(at8 == 1, dec_gain_row, 0.0))
    spread_start(4)

    for j in range(1, nd):
        near_copy(j, r * nd + lax.rem(d - j + nd, nd)).wait_recv()
        relay_copy(j, r).start()

    @pl.when(late)
    def _():
        spread_wait(2)
        weight_grads(1)

    near_copy(0, (1 - r) * nd + d).wait_recv()
    for j in range(1, nd):
        relay_copy(j, 1 - r).wait_recv()
    weight_grads(0)
    spread_wait(4)
    total = jnp.sum(gains[...], axis=0)
    width = out_ge.shape[1]
    piece = total[:, 0:width]
    for i in range(1, peers):
        piece = jnp.where(me == i, total[:, i * width : (i + 1) * width], piece)
    out_ge[...] = piece[0:1]
    out_gd[...] = piece[1:2]

    @pl.when(s > 0)
    def _():
        hop(1, -1).wait_send()
        hop(3, -1).wait_send()

    for j in range(nd):
        near_copy(j, me).wait_send()
    for j in range(1, nd):
        relay_copy(j, r).wait_send()


def write_kernel(*refs):
    sources, targets, sems = refs[:4], refs[4:8], refs[8]
    copies = [
        pltpu.make_async_copy(a, b, sems.at[i]) for i, (a, b) in enumerate(zip(sources, targets))
    ]
    for c in copies:
        c.start()
    for c in copies:
        c.wait()


def one_kernel(latent, enc_weight, dec_weight, enc_gain, dec_gain, out_grad):
    batches, frames, rows_here, columns, channels = latent.shape
    ns, nr, nd = (lax.axis_size(a) for a in ("section", "rows", "dp"))
    peers = nr * nd
    cells = frames * rows_here * nr * columns
    counted = cells * (channels // GROUPS)
    loss_scale = 1.0 / math.sqrt(batches * nd * cells)
    taps = 27 * channels
    share = taps // peers
    blocks = max(
        min((i * share + share - 1) // channels, 26) - i * share // channels + 1
        for i in range(peers)
    )
    owner = np.arange(channels) // (channels // GROUPS)
    groups = jnp.asarray(owner[:, None] == owner[None, :], BF16)
    field = pltpu.VMEM((cells, channels), BF16)
    wide = pltpu.VMEM((cells, channels), F32)
    weights = pltpu.VMEM((taps, channels), BF16)
    turned = pltpu.VMEM((channels, taps), BF16)
    every = pltpu.VMEM((peers, cells, channels), BF16)
    vector = pltpu.VMEM((1, channels), F32)
    vmem = pl.BlockSpec(memory_space=pltpu.VMEM)
    anywhere = pl.BlockSpec(memory_space=pl.ANY)
    dma = pltpu.SemaphoreType.DMA
    flops = 2 * cells * taps * channels * 4 + 4 * share * peers * cells * channels
    grads = jax.ShapeDtypeStruct((1, channels, share), F32)
    gain_grads = jax.ShapeDtypeStruct((1, channels // peers), F32)
    shapes = (grads, grads, gain_grads, gain_grads)
    results = pl.pallas_call(
        functools.partial(level_kernel, (ns, nr, nd), float(counted), loss_scale, blocks),
        out_shape=shapes,
        in_specs=[vmem, vmem, anywhere, anywhere, vmem, vmem, vmem],
        out_specs=(vmem, vmem, vmem, vmem),
        scratch_shapes=[
            turned, turned, weights, weights, weights, weights,
            pltpu.VMEM((2, cells // 2, channels), BF16),
            pltpu.VMEM((2, cells // 2, channels), BF16),
            field, field, field, field, field, field, field, field, field,
            wide, wide, wide, wide, wide, wide, vector, vector,
            every, every, every, every,
            pltpu.VMEM((peers, 8, channels), F32),
            pltpu.VMEM((blocks, channels, peers * cells), BF16),
            pltpu.VMEM((blocks, channels, peers * cells), BF16),
            pltpu.VMEM((blocks * channels, channels), F32),
            dma((2,)), dma((4,)), dma((4,)), dma((2,)), dma((2,)),
            dma((5, peers)), dma((5, peers)),
        ],
        compiler_params=pltpu.CompilerParams(
            collective_id=0, has_side_effects=True, vmem_limit_bytes=48 * 1024 * 1024
        ),
        cost_estimate=pl.CostEstimate(
            flops=flops, bytes_accessed=4 * taps * channels, transcendentals=4 * cells * channels
        ),
    )(
        latent, out_grad, jnp.swapaxes(enc_weight, 1, 2), jnp.swapaxes(dec_weight, 1, 2),
        enc_gain, dec_gain, groups,
    )
    enc, dec, enc_g, dec_g = pl.pallas_call(
        write_kernel,
        out_shape=shapes,
        in_specs=[vmem] * 4,
        out_specs=(anywhere,) * 4,
        scratch_shapes=[dma((4,))],
    )(*results)
    return (jnp.swapaxes(enc, 1, 2), jnp.swapaxes(dec, 1, 2), enc_g, dec_g)


def per_device(latent, *rest):
    batches, frames, rows_here, columns, channels = latent.shape
    rows, dp = lax.axis_size("rows"), lax.axis_size("dp")
    taps = 27 * channels
    fits = (
        rows == 2 and batches == 2 and frames == 2 and columns == 8 and rows_here % 4 == 0
        and rows_here * rows * 16 == 128
        and taps % (8 * rows * dp) == 0 and channels % 64 == 0 and channels % (rows * dp) == 0
        and lax.axis_size("section") > 1
    )
    return (one_kernel if fits else on_device)(latent, *rest)


def solution(mesh):
    in_specs = (
        P("dp", None, "rows", None, None),
        P("section", None, None),
        P("section", None, None),
        P("section", None),
        P("section", None),
        P("dp", None, "rows", None, None),
    )
    out_specs = (
        P("section", ("rows", "dp"), None),
        P("section", ("rows", "dp"), None),
        P("section", ("rows", "dp")),
        P("section", ("rows", "dp")),
    )
    return jax.shard_map(
        per_device, mesh=mesh, in_specs=in_specs, out_specs=out_specs, check_vma=False
    )
```

```python
import functools
import math

import jax
import jax.numpy as jnp
from jax import lax
from jax.experimental import pallas as pl
from jax.experimental.pallas import tpu as pltpu
from jax.sharding import PartitionSpec as P

GROUPS = 32


EPSILON = 1e-05


def padded_2(block, sides, width):
    for axis, dim in sides:
        count = lax.axis_size(axis)
        forward = [(i, i + 1) for i in range(count - 1)]
        backward = [(target, source) for source, target in forward]
        low = lax.ppermute(
            lax.slice_in_dim(block, block.shape[dim] - width, None, axis=dim), axis, forward
        )
        high = lax.ppermute(lax.slice_in_dim(block, 0, width, axis=dim), axis, backward)
        block = jnp.concatenate([low, block, high], axis=dim)
    return block


def passed_along(block, axis, distance):
    devices = range(lax.axis_size(axis))
    route = [(i - distance, i) for i in devices if i - distance in devices]
    return lax.ppermute(block, axis, route)


def spread_groups(values, channels):
    return jnp.repeat(values, channels // GROUPS)


def gather_patches(grown_rows):
    frames, padded_rows, columns, channels = grown_rows.shape
    inner_rows = padded_rows - 2
    padded = jnp.pad(grown_rows, ((1, 1), (0, 0), (1, 1), (0, 0)))
    pieces = []
    for lag_frame in range(3):
        for lag_row in range(3):
            for lag_column in range(3):
                pieces.append(
                    padded[
                        lag_frame : lag_frame + frames,
                        lag_row : lag_row + inner_rows,
                        lag_column : lag_column + columns,
                        :,
                    ]
                )
    return jnp.concatenate(pieces, axis=-1).reshape(frames * inner_rows * columns, 27 * channels)


def flipped(weights):
    channels = weights.shape[1]
    blocks = weights.reshape(27, -1, channels)[::-1]
    return jnp.swapaxes(blocks, 1, 2).reshape(-1, blocks.shape[1])


def take_slot(buffer, slot_index):
    return lax.dynamic_index_in_dim(buffer, slot_index, 0, keepdims=False)


def store_slot(buffer, slot_index, valid_now, new_value):
    kept = jnp.where(valid_now, new_value, take_slot(buffer, slot_index))
    return lax.dynamic_update_index_in_dim(buffer, kept, slot_index, 0)


def weight_gradient(grown_all, cotangent_all):
    patches = jax.vmap(gather_patches)(grown_all)
    patches = patches.reshape(-1, patches.shape[-1])
    flat_cot = cotangent_all.reshape(-1, cotangent_all.shape[-1])
    return lax.dot_general(
        patches, flat_cot, (((0,), (0,)), ((), ())), preferred_element_type=jnp.float32
    )


def norm_stats(volume, counted):
    grouped = volume.reshape(-1, GROUPS, volume.shape[-1] // GROUPS)
    totals = lax.psum(jnp.sum(grouped, axis=(0, 2)), "rows")
    centre = totals / counted
    deviation = grouped - centre[None, :, None]
    spread = lax.psum(jnp.sum(deviation * deviation, axis=(0, 2)), "rows") / counted
    return (centre, lax.rsqrt(spread + EPSILON))


def forward_block(volume, gain_vec, weights, counted):
    channels = volume.shape[-1]
    centre, inverse = norm_stats(volume, counted)
    normed = (volume - spread_groups(centre, channels)) * spread_groups(inverse, channels)
    active = jax.nn.silu(normed * gain_vec).astype(jnp.bfloat16)
    grown_act = padded_2(active, (("rows", 1),), 1)
    conv_out = jnp.dot(gather_patches(grown_act), weights, preferred_element_type=jnp.float32)
    return (grown_act, centre, inverse, volume + conv_out.reshape(volume.shape))


def backward_block(volume, gain_vec, reverse_weights, centre, inverse, cotangent, counted):
    channels = volume.shape[-1]
    inverse_full = spread_groups(inverse, channels)
    normed = (volume - spread_groups(centre, channels)) * inverse_full
    zvalue = normed * gain_vec
    cotangent_low = cotangent.astype(jnp.bfloat16)
    grown_cot = padded_2(cotangent_low, (("rows", 1),), 1)
    act_grad = jnp.dot(
        gather_patches(grown_cot), reverse_weights, preferred_element_type=jnp.float32
    ).reshape(volume.shape)
    logistic = jax.nn.sigmoid(zvalue)
    pre_grad = act_grad * logistic * (1.0 + zvalue * (1.0 - logistic))
    hat_grad = pre_grad * gain_vec
    grouped_grad = hat_grad.reshape(-1, GROUPS, channels // GROUPS)
    grouped_hat = normed.reshape(-1, GROUPS, channels // GROUPS)
    first_sum, second_sum = lax.psum(
        (jnp.sum(grouped_grad, axis=(0, 2)), jnp.sum(grouped_grad * grouped_hat, axis=(0, 2))),
        "rows",
    )
    input_grad = inverse_full * (
        hat_grad
        - spread_groups(first_sum / counted, channels)
        - normed * spread_groups(second_sum / counted, channels)
    )
    gain_part = jnp.sum((pre_grad * normed).reshape(-1, channels), axis=0)
    return (cotangent + input_grad, cotangent_low, gain_part)


def on_device(latent, enc_weight, dec_weight, enc_gain, dec_gain, out_grad):
    section_pos = lax.axis_index("section")
    section_count = lax.axis_size("section")
    batches, frames, rows_here, columns, channels = latent.shape
    counted = frames * rows_here * columns * (channels // GROUPS) * lax.axis_size("rows")
    cells_all = batches * lax.axis_size("dp") * frames * rows_here * lax.axis_size("rows") * columns
    loss_scale = 1.0 / math.sqrt(cells_all)
    clock_len = batches + section_count - 1
    last_pos = section_count - 1
    grown_shape = (batches, frames, rows_here + 2, columns, channels)
    enc_inputs = jnp.zeros(latent.shape, jnp.bfloat16)
    enc_tops = jnp.zeros(latent.shape, jnp.bfloat16)
    enc_grown = jnp.zeros(grown_shape, jnp.bfloat16)
    enc_centre = jnp.zeros((batches, GROUPS), jnp.float32)
    enc_inverse = jnp.zeros((batches, GROUPS), jnp.float32)
    arriving = jnp.zeros(latent.shape[1:], jnp.bfloat16)
    for clock_step in range(clock_len):
        micro_index = clock_step - section_pos
        valid_now = (micro_index >= 0) & (micro_index < batches)
        slot_index = jnp.clip(micro_index, 0, batches - 1)
        entering = jnp.where(section_pos == 0, latent[min(clock_step, batches - 1)], arriving)
        grown_act, centre, inverse, result = forward_block(
            entering.astype(jnp.float32), enc_gain[0], enc_weight[0], counted
        )
        leaving = result.astype(jnp.bfloat16)
        enc_inputs = store_slot(enc_inputs, slot_index, valid_now, entering)
        enc_tops = store_slot(enc_tops, slot_index, valid_now, leaving)
        enc_grown = store_slot(enc_grown, slot_index, valid_now, grown_act)
        enc_centre = store_slot(enc_centre, slot_index, valid_now, centre)
        enc_inverse = store_slot(enc_inverse, slot_index, valid_now, inverse)
        if clock_step + 1 < clock_len:
            arriving = passed_along(leaving, "section", 1)
    dec_downs = jnp.zeros(latent.shape, jnp.bfloat16)
    dec_grown = jnp.zeros(grown_shape, jnp.bfloat16)
    dec_centre = jnp.zeros((batches, GROUPS), jnp.float32)
    dec_inverse = jnp.zeros((batches, GROUPS), jnp.float32)
    arriving = jnp.zeros(latent.shape[1:], jnp.bfloat16)
    for clock_step in range(clock_len):
        micro_index = clock_step - (last_pos - section_pos)
        valid_now = (micro_index >= 0) & (micro_index < batches)
        slot_index = jnp.clip(micro_index, 0, batches - 1)
        coming = jnp.where(section_pos == last_pos, take_slot(enc_tops, slot_index), arriving)
        united = coming.astype(jnp.float32) + take_slot(enc_inputs, slot_index).astype(jnp.float32)
        grown_act, centre, inverse, result = forward_block(
            united, dec_gain[0], dec_weight[0], counted
        )
        dec_downs = store_slot(dec_downs, slot_index, valid_now, coming)
        dec_grown = store_slot(dec_grown, slot_index, valid_now, grown_act)
        dec_centre = store_slot(dec_centre, slot_index, valid_now, centre)
        dec_inverse = store_slot(dec_inverse, slot_index, valid_now, inverse)
        if clock_step + 1 < clock_len:
            arriving = passed_along(result.astype(jnp.bfloat16), "section", -1)
    dec_reverse = flipped(dec_weight[0])
    skip_grads = jnp.zeros(latent.shape, jnp.float32)
    dec_cotangents = jnp.zeros(latent.shape, jnp.bfloat16)
    dec_gain_sum = jnp.zeros((channels,), jnp.float32)
    arriving_grad = jnp.zeros(latent.shape[1:], jnp.float32)
    for clock_step in range(clock_len):
        micro_index = clock_step - section_pos
        valid_now = (micro_index >= 0) & (micro_index < batches)
        slot_index = jnp.clip(micro_index, 0, batches - 1)
        seeded = out_grad[min(clock_step, batches - 1)].astype(jnp.float32) * loss_scale
        incoming = jnp.where(valid_now, jnp.where(section_pos == 0, seeded, arriving_grad), 0.0)
        united = take_slot(dec_downs, slot_index).astype(jnp.float32) + take_slot(
            enc_inputs, slot_index
        ).astype(jnp.float32)
        passed, cotangent_low, gain_part = backward_block(
            united,
            dec_gain[0],
            dec_reverse,
            take_slot(dec_centre, slot_index),
            take_slot(dec_inverse, slot_index),
            incoming,
            counted,
        )
        dec_gain_sum = dec_gain_sum + gain_part
        dec_cotangents = store_slot(dec_cotangents, slot_index, valid_now, cotangent_low)
        skip_grads = store_slot(skip_grads, slot_index, valid_now, passed)
        if clock_step + 1 < clock_len:
            arriving_grad = passed_along(passed.astype(jnp.bfloat16), "section", 1).astype(
                passed.dtype
            )
    dec_gradient = weight_gradient(dec_grown, dec_cotangents)
    enc_reverse = flipped(enc_weight[0])
    enc_cotangents = jnp.zeros(latent.shape, jnp.bfloat16)
    enc_gain_sum = jnp.zeros((channels,), jnp.float32)
    arriving_grad = jnp.zeros(latent.shape[1:], jnp.float32)
    for clock_step in range(clock_len):
        micro_index = clock_step - (last_pos - section_pos)
        valid_now = (micro_index >= 0) & (micro_index < batches)
        slot_index = jnp.clip(micro_index, 0, batches - 1)
        skip_here = take_slot(skip_grads, slot_index)
        incoming = jnp.where(
            valid_now, jnp.where(section_pos == last_pos, skip_here, arriving_grad), 0.0
        )
        volume = take_slot(enc_inputs, slot_index).astype(jnp.float32)
        passed, cotangent_low, gain_part = backward_block(
            volume,
            enc_gain[0],
            enc_reverse,
            take_slot(enc_centre, slot_index),
            take_slot(enc_inverse, slot_index),
            incoming,
            counted,
        )
        enc_gain_sum = enc_gain_sum + gain_part
        enc_cotangents = store_slot(enc_cotangents, slot_index, valid_now, cotangent_low)
        leaving_grad = passed + skip_here
        if clock_step + 1 < clock_len:
            arriving_grad = passed_along(leaving_grad.astype(jnp.bfloat16), "section", -1).astype(
                leaving_grad.dtype
            )
    enc_gradient = weight_gradient(enc_grown, enc_cotangents)
    weight_all, gain_all = (
        lax.psum_scatter(
            jnp.stack([enc_gradient, dec_gradient]), ("rows", "dp"), scatter_dimension=1, tiled=True
        ),
        lax.psum_scatter(
            jnp.stack([enc_gain_sum, dec_gain_sum]), ("rows", "dp"), scatter_dimension=1, tiled=True
        ),
    )
    enc_result = weight_all[0:1]
    dec_result = weight_all[1:2]
    enc_gains = gain_all[0:1]
    dec_gains = gain_all[1:2]
    return (enc_result, dec_result, enc_gains, dec_gains)

MESH = pl.DeviceIdType.MESH
F32, BF16 = jnp.float32, jnp.bfloat16


def level_kernel(
    dims, counted, loss_scale, blocks,
    lat_hbm, grad_hbm, we_hbm, wd_hbm, ge_hbm, gd_hbm,
    out_we, out_wd, out_ge, out_gd,
    lat, grad, ge, gd, group_ref,
    wt_e, wt_d, we, wd, we_rev, wd_rev, lat_cells, grad_cells,
    hin, din, ein, fin, hout, dout, eout, fout, yin,
    xhat_e, xhat_d, slope_e, slope_d, ga_s, skip, rstd_e, rstd_d,
    acts_e, acts_d, cots_e, cots_d, gains, vt_e, vt_d, gradient,
    w_sem, in_sem, hop_send, hop_recv, half_send, half_recv, all_send, all_recv,
):
    ns, nr, nd = dims
    channels = ge.shape[1]
    cells = hin.shape[0]
    half = cells // 2
    s, r, d = (lax.axis_index(a) for a in ("section", "rows", "dp"))
    last = ns - 1
    peers = nr * nd
    me = r * nd + d
    slot = d * nr + r

    def peer_id(k):
        p = lax.rem(slot + k, peers)
        return (s, lax.rem(p, nr), lax.div(p, nr))

    small = [
        pltpu.make_async_copy(a, b, in_sem.at[i])
        for i, (a, b) in enumerate(((lat_hbm, lat), (grad_hbm, grad), (ge_hbm, ge), (gd_hbm, gd)))
    ]
    small[0].start()
    small[2].start()

    def weight_copy(which):
        hbm, buf = ((we_hbm, wt_e), (wd_hbm, wt_d))[which]
        return pltpu.make_async_copy(hbm.at[0], buf, w_sem.at[which])

    weight_copy(0).start()
    weight_copy(1).start()
    small[1].start()
    small[3].start()

    barrier = pltpu.get_barrier_semaphore()
    for k in range(1, peers):
        pl.semaphore_signal(barrier, inc=1, device_id=peer_id(k), device_id_type=MESH)

    @pl.when(s > 0)
    def _():
        pl.semaphore_signal(barrier, inc=1, device_id=(s - 1, r, d), device_id_type=MESH)

    @pl.when(s < last)
    def _():
        pl.semaphore_signal(barrier, inc=1, device_id=(s + 1, r, d), device_id_type=MESH)

    def by_rows(ref):
        x = ref[...].astype(F32)
        x = jnp.stack([x[:, 0], x[:, 1]], axis=2)
        return x.reshape(2, half, channels).astype(BF16)

    size = channels // GROUPS
    own = [
        jnp.floor(
            (lax.broadcasted_iota(jnp.int32, (channels, channels), i).astype(F32) + 0.5) / size
        )
        for i in range(2)
    ]
    group_ref[...] = jnp.where(own[0] == own[1], 1.0, 0.0).astype(BF16)

    small[0].wait()
    lat_cells[...] = by_rows(lat)
    small[1].wait()
    grad_cells[...] = by_rows(grad)
    pl.semaphore_wait(barrier, peers - 1 + (s > 0).astype(jnp.int32) + (s < last).astype(jnp.int32))

    def half_copy(i):
        source, target = ((lat_cells, hin), (grad_cells, yin))[i]
        return pltpu.make_async_remote_copy(
            src_ref=source.at[1 - r],
            dst_ref=target.at[pl.ds(pl.multiple_of(r * half, half), half)],
            send_sem=half_send.at[i],
            recv_sem=half_recv.at[i],
            device_id=(s, 1 - r, d),
            device_id_type=MESH,
        )

    @pl.when(s == 0)
    def _():
        half_copy(0).start()
        half_copy(1).start()
        mine = pl.ds(pl.multiple_of(r * half, half), half)
        hin[mine, :] = lat_cells[r]
        yin[mine, :] = grad_cells[r]

    def hop(i, step):
        source, target = ((hout, hin), (dout, din), (eout, ein), (fout, fin))[i]
        return pltpu.make_async_remote_copy(
            src_ref=source,
            dst_ref=target,
            send_sem=hop_send.at[i],
            recv_sem=hop_recv.at[i],
            device_id=(lax.rem(s + step + ns, ns), r, d),
            device_id_type=MESH,
        )

    def spread_copy(kind, k, owner):
        buf = (acts_e, acts_d, cots_d, cots_e, gains)[kind]
        return pltpu.make_async_remote_copy(
            src_ref=buf.at[slot],
            dst_ref=buf.at[owner],
            send_sem=all_send.at[kind, k],
            recv_sem=all_recv.at[kind, k],
            device_id=peer_id(k),
            device_id_type=MESH,
        )

    def spread_start(kind):
        for k in range(1, peers):
            spread_copy(kind, k, slot).start()

    def spread_wait(kind):
        for k in range(1, peers):
            c = spread_copy(kind, k, lax.rem(slot - k + peers, peers))
            c.wait_send()
            c.wait_recv()

    row_at = lax.broadcasted_iota(jnp.int32, (16, channels), 0)

    def group_sums(vectors):
        stacked = jnp.zeros((16, channels), F32)
        at = 0
        for x in vectors:
            hi = x.astype(BF16).astype(F32)
            mid = (x - hi).astype(BF16).astype(F32)
            for part in (hi, mid, x - hi - mid):
                stacked = jnp.where(row_at == at, part, stacked)
                at += 1
        out = jnp.dot(stacked.astype(BF16), group_ref[...], preferred_element_type=F32)
        return [out[3 * i : 3 * i + 1] + out[3 * i + 1 : 3 * i + 2] + out[3 * i + 2 : 3 * i + 3]
                for i in range(len(vectors))]

    def cell_sum(x):
        return jnp.sum(x, axis=0, keepdims=True)

    col_at = lax.broadcasted_iota(jnp.int32, (cells // 8, 8, channels), 1)

    def conv(field, w_ref):
        v = field.reshape(cells // 8, 8, channels)
        zero = jnp.zeros_like(v)
        shifted = (
            jnp.where(col_at >= 1, pltpu.roll(v, 1, 1), zero),
            v,
            jnp.where(col_at <= 6, pltpu.roll(v, 7, 1), zero),
        )
        none = jnp.zeros((cells // 16, 1, 8, channels), F32)
        edge = jnp.zeros((16, channels), BF16)
        pieces = []
        for dt in range(3):
            framed = []
            for x in shifted:
                x = x.reshape(cells // 16, 2, 8, channels)
                if dt == 0:
                    x = jnp.concatenate([none, x[:, :1]], axis=1)
                elif dt == 2:
                    x = jnp.concatenate([x[:, 1:], none], axis=1)
                framed.append(x.reshape(cells, channels).astype(BF16))
            pieces += [jnp.concatenate([edge, x[: cells - 16]], axis=0) for x in framed]
            pieces += framed
            pieces += [jnp.concatenate([x[16:], edge], axis=0) for x in framed]
        total = jnp.zeros((cells, channels), F32)
        for at in range(0, 27, 4):
            chunk = pieces[at : at + 4]
            total = total + jnp.dot(
                jnp.concatenate(chunk, axis=1),
                w_ref[at * channels : (at + len(chunk)) * channels, :],
                preferred_element_type=F32,
            )
        return total

    def normed(x, gain, xhat_ref, rstd_ref, acts):
        (mean,) = group_sums([cell_sum(x)])
        x = x - mean / counted
        (spread,) = group_sums([cell_sum(x * x)])
        inverse = lax.rsqrt(spread / counted + EPSILON)
        xhat = x * inverse
        z = xhat * gain
        a = (z * jax.nn.sigmoid(z)).astype(BF16)
        xhat_ref[...] = xhat
        rstd_ref[...] = inverse
        acts[slot] = a
        return a.astype(F32)

    def slope(xhat_ref, gain, slope_ref):
        z = xhat_ref[...] * gain
        sg = jax.nn.sigmoid(z)
        slope_ref[...] = sg * (1.0 + z * (1.0 - sg))

    def turn_weights(source, target):
        step = 2 * channels
        whole = 27 * channels // step

        def turn(j, _):
            at = pl.ds(pl.multiple_of(j * step, step), step)
            target[at, :] = source[:, at].astype(F32).T.astype(BF16)
            return 0

        lax.fori_loop(0, whole, turn, 0)
        target[whole * step :, :] = source[:, whole * step :].astype(F32).T.astype(BF16)

    def reverse_weights(source, target):
        for o in range(27):
            target[(26 - o) * channels : (27 - o) * channels, :] = source[
                :, o * channels : (o + 1) * channels
            ]

    share = 27 * channels // peers
    first_block = lax.div(me * share, channels)

    def shifted_acts(kind):
        buf, target = ((acts_e, vt_e), (acts_d, vt_d))[kind]
        cell = lax.broadcasted_iota(jnp.int32, (cells, channels), 0)
        row, frame, col = cell >> 4, (cell >> 3) & 1, cell & 7
        rows_all = cells // 16

        for j in range(blocks):
            b = jnp.minimum(first_block + j, 26)
            dt, dh, dw = lax.div(b, 9) - 1, lax.rem(lax.div(b, 3), 3) - 1, lax.rem(b, 3) - 1
            turn = lax.rem(cells - (dh * 16 + dt * 8 + dw), cells)
            valid = (
                (row + dh >= 0) & (row + dh < rows_all)
                & (frame + dt >= 0) & (frame + dt < 2)
                & (col + dw >= 0) & (col + dw < 8)
            )

            def one(p, _, j=j, turn=turn, valid=valid):
                x = pltpu.roll(buf[p].astype(F32), turn, 0)
                x = jnp.where(valid, x, 0.0).T.astype(BF16)
                target[j, :, pl.ds(pl.multiple_of(p * cells, cells), cells)] = x
                return 0

            lax.fori_loop(0, peers, one, 0)

    pair = nr * cells

    def add_chip(kind, chip, first):
        cots, vt = ((cots_e, vt_e), (cots_d, vt_d))[kind]
        at = pl.ds(pl.multiple_of(chip * pair, pair), pair)
        flat = cots[pl.ds(chip * nr, nr)].reshape(pair, channels)
        for j in range(blocks):
            term = jnp.dot(vt[j, :, at], flat, preferred_element_type=F32)
            rows = slice(j * channels, (j + 1) * channels)
            gradient[rows, :] = term if first else gradient[rows, :] + term

    def write_grads(out):
        begin = pl.multiple_of(me * share - first_block * channels, 8)
        out[0] = gradient[pl.ds(begin, share), :].T

    def dec_weight_grads():
        flat = cots_d[...].reshape(peers * cells, channels)
        for j in range(blocks):
            gradient[j * channels : (j + 1) * channels, :] = jnp.dot(
                vt_d[j], flat, preferred_element_type=F32
            )
        write_grads(out_wd)

    def backward(ga, y, gain, xhat_ref, slope_ref, rstd_ref):
        gz = ga * slope_ref[...]
        xhat = xhat_ref[...]
        gx = gz * gain
        first, second = group_sums([cell_sum(gx), cell_sum(gx * xhat)])
        result = y + rstd_ref[...] * (gx - first / counted - xhat * (second / counted))
        return result, gz * xhat

    def near_copy(j, owner):
        if j == 0:
            to = (s, 1 - r, d)
        else:
            to = (s, r, lax.rem(d + j, nd))
        return pltpu.make_async_remote_copy(
            src_ref=cots_e.at[slot],
            dst_ref=cots_e.at[owner],
            send_sem=all_send.at[3, j],
            recv_sem=all_recv.at[3, j],
            device_id=to,
            device_id_type=MESH,
        )

    def relay_copy(j, core):
        owner = lax.rem(d - j + nd, nd) * nr + core
        return pltpu.make_async_remote_copy(
            src_ref=cots_e.at[owner],
            dst_ref=cots_e.at[owner],
            send_sem=all_send.at[3, nd - 1 + j],
            recv_sem=all_recv.at[3, nd - 1 + j],
            device_id=(s, 1 - r, d),
            device_id_type=MESH,
        )

    late = 2 * s >= ns
    small[2].wait()
    small[3].wait()

    weight_copy(0).wait()
    turn_weights(wt_e, we)

    @pl.when(s > 0)
    def _():
        weight_copy(1).wait()
        turn_weights(wt_d, wd)
        hop(0, -1).wait_recv()

    @pl.when(s == 0)
    def _():
        half_copy(0).wait()

    x = hin[...].astype(F32)
    result = x + conv(normed(x, ge[...], xhat_e, rstd_e, acts_e), we)
    h = result.astype(BF16)

    @pl.when(s < last)
    def _():
        hout[...] = h
        hop(0, 1).start()

    @pl.when(s == last)
    def _():
        din[...] = h

    spread_start(0)

    @pl.when(s == 0)
    def _():
        weight_copy(1).wait()

    def first_idle():
        slope(xhat_e, ge[...], slope_e)
        reverse_weights(wt_d, wd_rev)
        reverse_weights(wt_e, we_rev)

        @pl.when(s == 0)
        def _():
            half_copy(1).wait()
            y = yin[...].astype(F32) * loss_scale
            yb = y.astype(BF16)
            cots_d[slot] = yb
            ga_s[...] = conv(yb.astype(F32), wd_rev)
            spread_start(2)

        spread_wait(0)
        shifted_acts(0)

    @pl.when(jnp.logical_not(late))
    def _():
        first_idle()

    @pl.when(s < last)
    def _():
        hop(0, 1).wait_send()
        hop(1, 1).wait_recv()

    u = din[...].astype(F32) + hin[...].astype(F32)
    a = normed(u, gd[...], xhat_d, rstd_d, acts_d)

    @pl.when(s > 0)
    def _():
        dout[...] = (u + conv(a, wd)).astype(BF16)
        hop(1, -1).start()
        spread_start(1)

    slope(xhat_d, gd[...], slope_d)

    @pl.when(late)
    def _():
        first_idle()
        spread_wait(1)
        shifted_acts(1)

    @pl.when(s > 0)
    def _():
        hop(2, -1).wait_recv()
        yb = ein[...]
        cots_d[slot] = yb
        ga_s[...] = conv(yb.astype(F32), wd_rev)
        yin[...] = yb

    y = jnp.where(s == 0, loss_scale, 1.0) * yin[...].astype(F32)
    c, gain_cells = backward(ga_s[...], y, gd[...], xhat_d, slope_d, rstd_d)
    skip[...] = c

    @pl.when(s < last)
    def _():
        eout[...] = c.astype(BF16)
        hop(2, 1).start()

    dec_gain_row = cell_sum(gain_cells)

    @pl.when(s == 0)
    def _():
        spread_start(1)

    @pl.when(s > 0)
    def _():
        spread_start(2)

    @pl.when(jnp.logical_not(late))
    def _():
        spread_wait(1)
        shifted_acts(1)
        spread_wait(2)
        dec_weight_grads()

    @pl.when(s < last)
    def _():
        hop(2, 1).wait_send()
        hop(3, 1).wait_recv()

    c = skip[...]
    y = jnp.where(s == last, c, fin[...].astype(F32))
    yb = y.astype(BF16)
    cots_e[slot] = yb
    for j in range(nd - 1, -1, -1):
        near_copy(j, slot).start()
    ga = conv(yb.astype(F32), we_rev)
    f, gain_cells = backward(ga, y, ge[...], xhat_e, slope_e, rstd_e)

    @pl.when(s > 0)
    def _():
        fout[...] = (f + c).astype(BF16)
        hop(3, -1).start()

    enc_gain_row = cell_sum(gain_cells)
    at8 = lax.broadcasted_iota(jnp.int32, (8, channels), 0)
    gains[slot] = jnp.where(at8 == 0, enc_gain_row, jnp.where(at8 == 1, dec_gain_row, 0.0))
    spread_start(4)

    for j in range(1, nd):
        near_copy(j, lax.rem(d - j + nd, nd) * nr + r).wait_recv()
        relay_copy(j, r).start()

    @pl.when(late)
    def _():
        spread_wait(2)
        dec_weight_grads()

    near_copy(0, d * nr + 1 - r).wait_recv()
    add_chip(0, d, True)
    for j in range(1, nd):
        relay_copy(j, 1 - r).wait_recv()
        add_chip(0, lax.rem(d - j + nd, nd), False)
    write_grads(out_we)
    spread_wait(4)
    total = jnp.sum(gains[...], axis=0)
    width = out_ge.shape[1]
    piece = total[:, 0:width]
    for i in range(1, peers):
        piece = jnp.where(me == i, total[:, i * width : (i + 1) * width], piece)
    out_ge[...] = piece[0:1]
    out_gd[...] = piece[1:2]

    @pl.when(s > 0)
    def _():
        hop(1, -1).wait_send()
        hop(3, -1).wait_send()

    for j in range(nd):
        near_copy(j, slot).wait_send()
    for j in range(1, nd):
        relay_copy(j, r).wait_send()


def write_kernel(*refs):
    sources, targets, sems = refs[:4], refs[4:8], refs[8]
    copies = [
        pltpu.make_async_copy(a, b, sems.at[i]) for i, (a, b) in enumerate(zip(sources, targets))
    ]
    for c in copies:
        c.start()
    for c in copies:
        c.wait()


def one_kernel(latent, enc_weight, dec_weight, enc_gain, dec_gain, out_grad):
    batches, frames, rows_here, columns, channels = latent.shape
    ns, nr, nd = (lax.axis_size(a) for a in ("section", "rows", "dp"))
    peers = nr * nd
    cells = frames * rows_here * nr * columns
    counted = cells * (channels // GROUPS)
    loss_scale = 1.0 / math.sqrt(batches * nd * cells)
    taps = 27 * channels
    share = taps // peers
    blocks = max(
        min((i * share + share - 1) // channels, 26) - i * share // channels + 1
        for i in range(peers)
    )
    field = pltpu.VMEM((cells, channels), BF16)
    wide = pltpu.VMEM((cells, channels), F32)
    weights = pltpu.VMEM((taps, channels), BF16)
    turned = pltpu.VMEM((channels, taps), BF16)
    every = pltpu.VMEM((peers, cells, channels), BF16)
    vector = pltpu.VMEM((1, channels), F32)
    vmem = pl.BlockSpec(memory_space=pltpu.VMEM)
    anywhere = pl.BlockSpec(memory_space=pl.ANY)
    far = pl.BlockSpec(memory_space=pltpu.HBM)
    part = pltpu.VMEM(latent.shape, BF16)
    dma = pltpu.SemaphoreType.DMA
    flops = 2 * cells * taps * channels * 4 + 4 * share * peers * cells * channels
    grads = jax.ShapeDtypeStruct((1, channels, share), F32)
    gain_grads = jax.ShapeDtypeStruct((1, channels // peers), F32)
    shapes = (grads, grads, gain_grads, gain_grads)
    results = pl.pallas_call(
        functools.partial(level_kernel, (ns, nr, nd), float(counted), loss_scale, blocks),
        out_shape=shapes,
        in_specs=[far] * 6,
        out_specs=(vmem, vmem, vmem, vmem),
        scratch_shapes=[
            part, part, vector, vector, pltpu.VMEM((channels, channels), BF16),
            turned, turned, weights, weights, weights, weights,
            pltpu.VMEM((2, cells // 2, channels), BF16),
            pltpu.VMEM((2, cells // 2, channels), BF16),
            field, field, field, field, field, field, field, field, field,
            wide, wide, wide, wide, wide, wide, vector, vector,
            every, every, every, every,
            pltpu.VMEM((peers, 8, channels), F32),
            pltpu.VMEM((blocks, channels, peers * cells), BF16),
            pltpu.VMEM((blocks, channels, peers * cells), BF16),
            pltpu.VMEM((blocks * channels, channels), F32),
            dma((2,)), dma((4,)), dma((4,)), dma((4,)), dma((2,)), dma((2,)),
            dma((5, peers)), dma((5, peers)),
        ],
        compiler_params=pltpu.CompilerParams(
            collective_id=0, has_side_effects=True, vmem_limit_bytes=62 * 1024 * 1024
        ),
        cost_estimate=pl.CostEstimate(
            flops=flops, bytes_accessed=4 * taps * channels, transcendentals=4 * cells * channels
        ),
    )(
        latent, out_grad, jnp.swapaxes(enc_weight, 1, 2), jnp.swapaxes(dec_weight, 1, 2),
        enc_gain, dec_gain,
    )
    enc, dec, enc_g, dec_g = pl.pallas_call(
        write_kernel,
        out_shape=shapes,
        in_specs=[anywhere] * 4,
        out_specs=(anywhere,) * 4,
        scratch_shapes=[dma((4,))],
        compiler_params=pltpu.CompilerParams(vmem_limit_bytes=62 * 1024 * 1024),
    )(*results)
    return (jnp.swapaxes(enc, 1, 2), jnp.swapaxes(dec, 1, 2), enc_g, dec_g)


def per_device(latent, *rest):
    batches, frames, rows_here, columns, channels = latent.shape
    rows, dp = lax.axis_size("rows"), lax.axis_size("dp")
    taps = 27 * channels
    fits = (
        rows == 2 and batches == 2 and frames == 2 and columns == 8 and rows_here % 4 == 0
        and rows_here * rows * 16 == 128
        and taps % (8 * rows * dp) == 0 and channels % 64 == 0 and channels % (rows * dp) == 0
        and lax.axis_size("section") > 1
    )
    return (one_kernel if fits else on_device)(latent, *rest)


def solution(mesh):
    in_specs = (
        P("dp", None, "rows", None, None),
        P("section", None, None),
        P("section", None, None),
        P("section", None),
        P("section", None),
        P("dp", None, "rows", None, None),
    )
    out_specs = (
        P("section", ("rows", "dp"), None),
        P("section", ("rows", "dp"), None),
        P("section", ("rows", "dp")),
        P("section", ("rows", "dp")),
    )
    return jax.shard_map(
        per_device, mesh=mesh, in_specs=in_specs, out_specs=out_specs, check_vma=False
    )
```

```python
import functools
import math

import jax
import jax.numpy as jnp
from jax import lax
from jax.experimental import pallas as pl
from jax.experimental.pallas import tpu as pltpu
from jax.sharding import PartitionSpec as P

GROUPS = 32


EPSILON = 1e-05


def padded_2(block, sides, width):
    for axis, dim in sides:
        count = lax.axis_size(axis)
        forward = [(i, i + 1) for i in range(count - 1)]
        backward = [(target, source) for source, target in forward]
        low = lax.ppermute(
            lax.slice_in_dim(block, block.shape[dim] - width, None, axis=dim), axis, forward
        )
        high = lax.ppermute(lax.slice_in_dim(block, 0, width, axis=dim), axis, backward)
        block = jnp.concatenate([low, block, high], axis=dim)
    return block


def passed_along(block, axis, distance):
    devices = range(lax.axis_size(axis))
    route = [(i - distance, i) for i in devices if i - distance in devices]
    return lax.ppermute(block, axis, route)


def spread_groups(values, channels):
    return jnp.repeat(values, channels // GROUPS)


def gather_patches(grown_rows):
    frames, padded_rows, columns, channels = grown_rows.shape
    inner_rows = padded_rows - 2
    padded = jnp.pad(grown_rows, ((1, 1), (0, 0), (1, 1), (0, 0)))
    pieces = []
    for lag_frame in range(3):
        for lag_row in range(3):
            for lag_column in range(3):
                pieces.append(
                    padded[
                        lag_frame : lag_frame + frames,
                        lag_row : lag_row + inner_rows,
                        lag_column : lag_column + columns,
                        :,
                    ]
                )
    return jnp.concatenate(pieces, axis=-1).reshape(frames * inner_rows * columns, 27 * channels)


def flipped(weights):
    channels = weights.shape[1]
    blocks = weights.reshape(27, -1, channels)[::-1]
    return jnp.swapaxes(blocks, 1, 2).reshape(-1, blocks.shape[1])


def take_slot(buffer, slot_index):
    return lax.dynamic_index_in_dim(buffer, slot_index, 0, keepdims=False)


def store_slot(buffer, slot_index, valid_now, new_value):
    kept = jnp.where(valid_now, new_value, take_slot(buffer, slot_index))
    return lax.dynamic_update_index_in_dim(buffer, kept, slot_index, 0)


def weight_gradient(grown_all, cotangent_all):
    patches = jax.vmap(gather_patches)(grown_all)
    patches = patches.reshape(-1, patches.shape[-1])
    flat_cot = cotangent_all.reshape(-1, cotangent_all.shape[-1])
    return lax.dot_general(
        patches, flat_cot, (((0,), (0,)), ((), ())), preferred_element_type=jnp.float32
    )


def norm_stats(volume, counted):
    grouped = volume.reshape(-1, GROUPS, volume.shape[-1] // GROUPS)
    totals = lax.psum(jnp.sum(grouped, axis=(0, 2)), "rows")
    centre = totals / counted
    deviation = grouped - centre[None, :, None]
    spread = lax.psum(jnp.sum(deviation * deviation, axis=(0, 2)), "rows") / counted
    return (centre, lax.rsqrt(spread + EPSILON))


def forward_block(volume, gain_vec, weights, counted):
    channels = volume.shape[-1]
    centre, inverse = norm_stats(volume, counted)
    normed = (volume - spread_groups(centre, channels)) * spread_groups(inverse, channels)
    active = jax.nn.silu(normed * gain_vec).astype(jnp.bfloat16)
    grown_act = padded_2(active, (("rows", 1),), 1)
    conv_out = jnp.dot(gather_patches(grown_act), weights, preferred_element_type=jnp.float32)
    return (grown_act, centre, inverse, volume + conv_out.reshape(volume.shape))


def backward_block(volume, gain_vec, reverse_weights, centre, inverse, cotangent, counted):
    channels = volume.shape[-1]
    inverse_full = spread_groups(inverse, channels)
    normed = (volume - spread_groups(centre, channels)) * inverse_full
    zvalue = normed * gain_vec
    cotangent_low = cotangent.astype(jnp.bfloat16)
    grown_cot = padded_2(cotangent_low, (("rows", 1),), 1)
    act_grad = jnp.dot(
        gather_patches(grown_cot), reverse_weights, preferred_element_type=jnp.float32
    ).reshape(volume.shape)
    logistic = jax.nn.sigmoid(zvalue)
    pre_grad = act_grad * logistic * (1.0 + zvalue * (1.0 - logistic))
    hat_grad = pre_grad * gain_vec
    grouped_grad = hat_grad.reshape(-1, GROUPS, channels // GROUPS)
    grouped_hat = normed.reshape(-1, GROUPS, channels // GROUPS)
    first_sum, second_sum = lax.psum(
        (jnp.sum(grouped_grad, axis=(0, 2)), jnp.sum(grouped_grad * grouped_hat, axis=(0, 2))),
        "rows",
    )
    input_grad = inverse_full * (
        hat_grad
        - spread_groups(first_sum / counted, channels)
        - normed * spread_groups(second_sum / counted, channels)
    )
    gain_part = jnp.sum((pre_grad * normed).reshape(-1, channels), axis=0)
    return (cotangent + input_grad, cotangent_low, gain_part)


def on_device(latent, enc_weight, dec_weight, enc_gain, dec_gain, out_grad):
    section_pos = lax.axis_index("section")
    section_count = lax.axis_size("section")
    batches, frames, rows_here, columns, channels = latent.shape
    counted = frames * rows_here * columns * (channels // GROUPS) * lax.axis_size("rows")
    cells_all = batches * lax.axis_size("dp") * frames * rows_here * lax.axis_size("rows") * columns
    loss_scale = 1.0 / math.sqrt(cells_all)
    clock_len = batches + section_count - 1
    last_pos = section_count - 1
    grown_shape = (batches, frames, rows_here + 2, columns, channels)
    enc_inputs = jnp.zeros(latent.shape, jnp.bfloat16)
    enc_tops = jnp.zeros(latent.shape, jnp.bfloat16)
    enc_grown = jnp.zeros(grown_shape, jnp.bfloat16)
    enc_centre = jnp.zeros((batches, GROUPS), jnp.float32)
    enc_inverse = jnp.zeros((batches, GROUPS), jnp.float32)
    arriving = jnp.zeros(latent.shape[1:], jnp.bfloat16)
    for clock_step in range(clock_len):
        micro_index = clock_step - section_pos
        valid_now = (micro_index >= 0) & (micro_index < batches)
        slot_index = jnp.clip(micro_index, 0, batches - 1)
        entering = jnp.where(section_pos == 0, latent[min(clock_step, batches - 1)], arriving)
        grown_act, centre, inverse, result = forward_block(
            entering.astype(jnp.float32), enc_gain[0], enc_weight[0], counted
        )
        leaving = result.astype(jnp.bfloat16)
        enc_inputs = store_slot(enc_inputs, slot_index, valid_now, entering)
        enc_tops = store_slot(enc_tops, slot_index, valid_now, leaving)
        enc_grown = store_slot(enc_grown, slot_index, valid_now, grown_act)
        enc_centre = store_slot(enc_centre, slot_index, valid_now, centre)
        enc_inverse = store_slot(enc_inverse, slot_index, valid_now, inverse)
        if clock_step + 1 < clock_len:
            arriving = passed_along(leaving, "section", 1)
    dec_downs = jnp.zeros(latent.shape, jnp.bfloat16)
    dec_grown = jnp.zeros(grown_shape, jnp.bfloat16)
    dec_centre = jnp.zeros((batches, GROUPS), jnp.float32)
    dec_inverse = jnp.zeros((batches, GROUPS), jnp.float32)
    arriving = jnp.zeros(latent.shape[1:], jnp.bfloat16)
    for clock_step in range(clock_len):
        micro_index = clock_step - (last_pos - section_pos)
        valid_now = (micro_index >= 0) & (micro_index < batches)
        slot_index = jnp.clip(micro_index, 0, batches - 1)
        coming = jnp.where(section_pos == last_pos, take_slot(enc_tops, slot_index), arriving)
        united = coming.astype(jnp.float32) + take_slot(enc_inputs, slot_index).astype(jnp.float32)
        grown_act, centre, inverse, result = forward_block(
            united, dec_gain[0], dec_weight[0], counted
        )
        dec_downs = store_slot(dec_downs, slot_index, valid_now, coming)
        dec_grown = store_slot(dec_grown, slot_index, valid_now, grown_act)
        dec_centre = store_slot(dec_centre, slot_index, valid_now, centre)
        dec_inverse = store_slot(dec_inverse, slot_index, valid_now, inverse)
        if clock_step + 1 < clock_len:
            arriving = passed_along(result.astype(jnp.bfloat16), "section", -1)
    dec_reverse = flipped(dec_weight[0])
    skip_grads = jnp.zeros(latent.shape, jnp.float32)
    dec_cotangents = jnp.zeros(latent.shape, jnp.bfloat16)
    dec_gain_sum = jnp.zeros((channels,), jnp.float32)
    arriving_grad = jnp.zeros(latent.shape[1:], jnp.float32)
    for clock_step in range(clock_len):
        micro_index = clock_step - section_pos
        valid_now = (micro_index >= 0) & (micro_index < batches)
        slot_index = jnp.clip(micro_index, 0, batches - 1)
        seeded = out_grad[min(clock_step, batches - 1)].astype(jnp.float32) * loss_scale
        incoming = jnp.where(valid_now, jnp.where(section_pos == 0, seeded, arriving_grad), 0.0)
        united = take_slot(dec_downs, slot_index).astype(jnp.float32) + take_slot(
            enc_inputs, slot_index
        ).astype(jnp.float32)
        passed, cotangent_low, gain_part = backward_block(
            united,
            dec_gain[0],
            dec_reverse,
            take_slot(dec_centre, slot_index),
            take_slot(dec_inverse, slot_index),
            incoming,
            counted,
        )
        dec_gain_sum = dec_gain_sum + gain_part
        dec_cotangents = store_slot(dec_cotangents, slot_index, valid_now, cotangent_low)
        skip_grads = store_slot(skip_grads, slot_index, valid_now, passed)
        if clock_step + 1 < clock_len:
            arriving_grad = passed_along(passed.astype(jnp.bfloat16), "section", 1).astype(
                passed.dtype
            )
    dec_gradient = weight_gradient(dec_grown, dec_cotangents)
    enc_reverse = flipped(enc_weight[0])
    enc_cotangents = jnp.zeros(latent.shape, jnp.bfloat16)
    enc_gain_sum = jnp.zeros((channels,), jnp.float32)
    arriving_grad = jnp.zeros(latent.shape[1:], jnp.float32)
    for clock_step in range(clock_len):
        micro_index = clock_step - (last_pos - section_pos)
        valid_now = (micro_index >= 0) & (micro_index < batches)
        slot_index = jnp.clip(micro_index, 0, batches - 1)
        skip_here = take_slot(skip_grads, slot_index)
        incoming = jnp.where(
            valid_now, jnp.where(section_pos == last_pos, skip_here, arriving_grad), 0.0
        )
        volume = take_slot(enc_inputs, slot_index).astype(jnp.float32)
        passed, cotangent_low, gain_part = backward_block(
            volume,
            enc_gain[0],
            enc_reverse,
            take_slot(enc_centre, slot_index),
            take_slot(enc_inverse, slot_index),
            incoming,
            counted,
        )
        enc_gain_sum = enc_gain_sum + gain_part
        enc_cotangents = store_slot(enc_cotangents, slot_index, valid_now, cotangent_low)
        leaving_grad = passed + skip_here
        if clock_step + 1 < clock_len:
            arriving_grad = passed_along(leaving_grad.astype(jnp.bfloat16), "section", -1).astype(
                leaving_grad.dtype
            )
    enc_gradient = weight_gradient(enc_grown, enc_cotangents)
    weight_all, gain_all = (
        lax.psum_scatter(
            jnp.stack([enc_gradient, dec_gradient]), ("rows", "dp"), scatter_dimension=1, tiled=True
        ),
        lax.psum_scatter(
            jnp.stack([enc_gain_sum, dec_gain_sum]), ("rows", "dp"), scatter_dimension=1, tiled=True
        ),
    )
    enc_result = weight_all[0:1]
    dec_result = weight_all[1:2]
    enc_gains = gain_all[0:1]
    dec_gains = gain_all[1:2]
    return (enc_result, dec_result, enc_gains, dec_gains)

MESH = pl.DeviceIdType.MESH
F32, BF16 = jnp.float32, jnp.bfloat16


def level_kernel(
    dims, counted, loss_scale, blocks,
    lat_hbm, grad_hbm, we_hbm, wd_hbm, ge_hbm, gd_hbm,
    out_we, out_wd, out_ge, out_gd,
    lat, grad, ge, gd, group_ref,
    wt_e, wt_d, we, wd, we_rev, wd_rev, lat_cells, grad_cells,
    hin, din, ein, fin, hout, dout, eout, fout, yin,
    xhat_e, xhat_d, slope_e, slope_d, ga_s, skip, rstd_e, rstd_d,
    acts_e, acts_d, cots_e, cots_d, gains, vt_e, vt_d, gradient,
    w_sem, in_sem, hop_send, hop_recv, half_send, half_recv, all_send, all_recv,
):
    ns, nr, nd = dims
    channels = ge.shape[1]
    cells = hin.shape[0]
    half = cells // 2
    s, r, d = (lax.axis_index(a) for a in ("section", "rows", "dp"))
    last = ns - 1
    peers = nr * nd
    me = r * nd + d
    slot = d * nr + r

    def peer_id(k):
        p = lax.rem(slot + k, peers)
        return (s, lax.rem(p, nr), lax.div(p, nr))

    small = [
        pltpu.make_async_copy(a, b, in_sem.at[i])
        for i, (a, b) in enumerate(((lat_hbm, lat), (grad_hbm, grad), (ge_hbm, ge), (gd_hbm, gd)))
    ]
    small[0].start()
    small[2].start()

    def weight_copy(which):
        hbm, buf = ((we_hbm, wt_e), (wd_hbm, wt_d))[which]
        return pltpu.make_async_copy(hbm.at[0], buf, w_sem.at[which])

    weight_copy(0).start()
    weight_copy(1).start()
    small[1].start()
    small[3].start()

    barrier = pltpu.get_barrier_semaphore()
    for k in range(1, peers):
        pl.semaphore_signal(barrier, inc=1, device_id=peer_id(k), device_id_type=MESH)

    @pl.when(s > 0)
    def _():
        pl.semaphore_signal(barrier, inc=1, device_id=(s - 1, r, d), device_id_type=MESH)

    @pl.when(s < last)
    def _():
        pl.semaphore_signal(barrier, inc=1, device_id=(s + 1, r, d), device_id_type=MESH)

    def by_rows(ref):
        x = ref[...].astype(F32)
        x = jnp.stack([x[:, 0], x[:, 1]], axis=2)
        return x.reshape(2, half, channels).astype(BF16)

    size = channels // GROUPS
    own = [
        jnp.floor(
            (lax.broadcasted_iota(jnp.int32, (channels, channels), i).astype(F32) + 0.5) / size
        )
        for i in range(2)
    ]
    group_ref[...] = jnp.where(own[0] == own[1], 1.0, 0.0).astype(BF16)

    small[0].wait()
    lat_cells[...] = by_rows(lat)
    small[1].wait()
    grad_cells[...] = by_rows(grad)
    pl.semaphore_wait(barrier, peers - 1 + (s > 0).astype(jnp.int32) + (s < last).astype(jnp.int32))

    def half_copy(i):
        source, target = ((lat_cells, hin), (grad_cells, yin))[i]
        return pltpu.make_async_remote_copy(
            src_ref=source.at[1 - r],
            dst_ref=target.at[pl.ds(pl.multiple_of(r * half, half), half)],
            send_sem=half_send.at[i],
            recv_sem=half_recv.at[i],
            device_id=(s, 1 - r, d),
            device_id_type=MESH,
        )

    @pl.when(s == 0)
    def _():
        half_copy(0).start()
        half_copy(1).start()
        mine = pl.ds(pl.multiple_of(r * half, half), half)
        hin[mine, :] = lat_cells[r]
        yin[mine, :] = grad_cells[r]

    def hop(i, step):
        source, target = ((hout, hin), (dout, din), (eout, ein), (fout, fin))[i]
        return pltpu.make_async_remote_copy(
            src_ref=source,
            dst_ref=target,
            send_sem=hop_send.at[i],
            recv_sem=hop_recv.at[i],
            device_id=(lax.rem(s + step + ns, ns), r, d),
            device_id_type=MESH,
        )

    def spread_copy(kind, k, owner):
        buf = (acts_e, acts_d, cots_d, cots_e, gains)[kind]
        return pltpu.make_async_remote_copy(
            src_ref=buf.at[slot],
            dst_ref=buf.at[owner],
            send_sem=all_send.at[kind, k],
            recv_sem=all_recv.at[kind, k],
            device_id=peer_id(k),
            device_id_type=MESH,
        )

    def spread_start(kind):
        for k in range(1, peers):
            spread_copy(kind, k, slot).start()

    def spread_wait(kind):
        for k in range(1, peers):
            c = spread_copy(kind, k, lax.rem(slot - k + peers, peers))
            c.wait_send()
            c.wait_recv()

    row_at = lax.broadcasted_iota(jnp.int32, (16, channels), 0)

    def group_sums(vectors):
        stacked = jnp.zeros((16, channels), F32)
        at = 0
        for x in vectors:
            hi = x.astype(BF16).astype(F32)
            mid = (x - hi).astype(BF16).astype(F32)
            for part in (hi, mid, x - hi - mid):
                stacked = jnp.where(row_at == at, part, stacked)
                at += 1
        out = jnp.dot(stacked.astype(BF16), group_ref[...], preferred_element_type=F32)
        return [out[3 * i : 3 * i + 1] + out[3 * i + 1 : 3 * i + 2] + out[3 * i + 2 : 3 * i + 3]
                for i in range(len(vectors))]

    def cell_sum(x):
        return jnp.sum(x, axis=0, keepdims=True)

    col_at = lax.broadcasted_iota(jnp.int32, (cells // 8, 8, channels), 1)

    def conv(field, w_ref):
        v = field.reshape(cells // 8, 8, channels)
        zero = jnp.zeros_like(v)
        shifted = (
            jnp.where(col_at >= 1, pltpu.roll(v, 1, 1), zero),
            v,
            jnp.where(col_at <= 6, pltpu.roll(v, 7, 1), zero),
        )
        none = jnp.zeros((cells // 16, 1, 8, channels), F32)
        edge = jnp.zeros((16, channels), BF16)
        pieces = []
        for dt in range(3):
            framed = []
            for x in shifted:
                x = x.reshape(cells // 16, 2, 8, channels)
                if dt == 0:
                    x = jnp.concatenate([none, x[:, :1]], axis=1)
                elif dt == 2:
                    x = jnp.concatenate([x[:, 1:], none], axis=1)
                framed.append(x.reshape(cells, channels).astype(BF16))
            pieces += [jnp.concatenate([edge, x[: cells - 16]], axis=0) for x in framed]
            pieces += framed
            pieces += [jnp.concatenate([x[16:], edge], axis=0) for x in framed]
        total = jnp.zeros((cells, channels), F32)
        for at in range(0, 27, 4):
            chunk = pieces[at : at + 4]
            total = total + jnp.dot(
                jnp.concatenate(chunk, axis=1),
                w_ref[at * channels : (at + len(chunk)) * channels, :],
                preferred_element_type=F32,
            )
        return total

    def normed(x, gain, xhat_ref, rstd_ref, acts):
        (mean,) = group_sums([cell_sum(x)])
        x = x - mean / counted
        (spread,) = group_sums([cell_sum(x * x)])
        inverse = lax.rsqrt(spread / counted + EPSILON)
        xhat = x * inverse
        z = xhat * gain
        a = (z * jax.nn.sigmoid(z)).astype(BF16)
        xhat_ref[...] = xhat
        rstd_ref[...] = inverse
        acts[slot] = a
        return a.astype(F32)

    def slope(xhat_ref, gain, slope_ref):
        z = xhat_ref[...] * gain
        sg = jax.nn.sigmoid(z)
        slope_ref[...] = sg * (1.0 + z * (1.0 - sg))

    def turn_weights(source, target):
        step = 2 * channels
        whole = 27 * channels // step

        def turn(j, _):
            at = pl.ds(pl.multiple_of(j * step, step), step)
            target[at, :] = source[:, at].astype(F32).T.astype(BF16)
            return 0

        lax.fori_loop(0, whole, turn, 0)
        target[whole * step :, :] = source[:, whole * step :].astype(F32).T.astype(BF16)

    def reverse_weights(source, target):
        for o in range(27):
            target[(26 - o) * channels : (27 - o) * channels, :] = source[
                :, o * channels : (o + 1) * channels
            ]

    share = 27 * channels // peers
    first_block = lax.div(me * share, channels)

    def shifted_acts(kind):
        buf, target = ((acts_e, vt_e), (acts_d, vt_d))[kind]
        cell = lax.broadcasted_iota(jnp.int32, (cells, channels), 0)
        row, frame, col = cell >> 4, (cell >> 3) & 1, cell & 7
        rows_all = cells // 16

        for j in range(blocks):
            b = jnp.minimum(first_block + j, 26)
            dt, dh, dw = lax.div(b, 9) - 1, lax.rem(lax.div(b, 3), 3) - 1, lax.rem(b, 3) - 1
            turn = lax.rem(cells - (dh * 16 + dt * 8 + dw), cells)
            valid = (
                (row + dh >= 0) & (row + dh < rows_all)
                & (frame + dt >= 0) & (frame + dt < 2)
                & (col + dw >= 0) & (col + dw < 8)
            )

            def one(p, _, j=j, turn=turn, valid=valid):
                x = pltpu.roll(buf[p].astype(F32), turn, 0)
                x = jnp.where(valid, x, 0.0).T.astype(BF16)
                target[j, :, pl.ds(pl.multiple_of(p * cells, cells), cells)] = x
                return 0

            lax.fori_loop(0, peers, one, 0)

    pair = nr * cells

    def add_chip(kind, chip, first):
        cots, vt = ((cots_e, vt_e), (cots_d, vt_d))[kind]
        at = pl.ds(pl.multiple_of(chip * pair, pair), pair)
        flat = cots[pl.ds(chip * nr, nr)].reshape(pair, channels)
        for j in range(blocks):
            term = jnp.dot(vt[j, :, at], flat, preferred_element_type=F32)
            rows = slice(j * channels, (j + 1) * channels)
            gradient[rows, :] = term if first else gradient[rows, :] + term

    def write_grads(out):
        begin = pl.multiple_of(me * share - first_block * channels, 8)
        out[0] = gradient[pl.ds(begin, share), :].T

    def dec_weight_grads():
        flat = cots_d[...].reshape(peers * cells, channels)
        for j in range(blocks):
            gradient[j * channels : (j + 1) * channels, :] = jnp.dot(
                vt_d[j], flat, preferred_element_type=F32
            )
        write_grads(out_wd)

    def backward(ga, y, gain, xhat_ref, slope_ref, rstd_ref):
        gz = ga * slope_ref[...]
        xhat = xhat_ref[...]
        gx = gz * gain
        first, second = group_sums([cell_sum(gx), cell_sum(gx * xhat)])
        result = y + rstd_ref[...] * (gx - first / counted - xhat * (second / counted))
        return result, gz * xhat

    def near_copy(j, owner):
        if j == 0:
            to = (s, 1 - r, d)
        else:
            to = (s, r, lax.rem(d + j, nd))
        return pltpu.make_async_remote_copy(
            src_ref=cots_e.at[slot],
            dst_ref=cots_e.at[owner],
            send_sem=all_send.at[3, j],
            recv_sem=all_recv.at[3, j],
            device_id=to,
            device_id_type=MESH,
        )

    def relay_copy(j, core):
        owner = lax.rem(d - j + nd, nd) * nr + core
        return pltpu.make_async_remote_copy(
            src_ref=cots_e.at[owner],
            dst_ref=cots_e.at[owner],
            send_sem=all_send.at[3, nd - 1 + j],
            recv_sem=all_recv.at[3, nd - 1 + j],
            device_id=(s, 1 - r, d),
            device_id_type=MESH,
        )

    late = 2 * s >= ns
    small[2].wait()
    small[3].wait()

    weight_copy(0).wait()
    turn_weights(wt_e, we)

    @pl.when(s > 0)
    def _():
        weight_copy(1).wait()
        turn_weights(wt_d, wd)
        hop(0, -1).wait_recv()

    @pl.when(s == 0)
    def _():
        half_copy(0).wait()

    x = hin[...].astype(F32)
    result = x + conv(normed(x, ge[...], xhat_e, rstd_e, acts_e), we)
    h = result.astype(BF16)

    @pl.when(s < last)
    def _():
        hout[...] = h
        hop(0, 1).start()

    @pl.when(s == last)
    def _():
        din[...] = h

    spread_start(0)

    @pl.when(s == 0)
    def _():
        weight_copy(1).wait()

    def first_idle():
        slope(xhat_e, ge[...], slope_e)
        reverse_weights(wt_d, wd_rev)
        reverse_weights(wt_e, we_rev)

        @pl.when(s == 0)
        def _():
            half_copy(1).wait()
            y = yin[...].astype(F32) * loss_scale
            yb = y.astype(BF16)
            cots_d[slot] = yb
            ga_s[...] = conv(yb.astype(F32), wd_rev)
            spread_start(2)

        spread_wait(0)
        shifted_acts(0)

    @pl.when(jnp.logical_not(late))
    def _():
        first_idle()

    @pl.when(s < last)
    def _():
        hop(0, 1).wait_send()
        hop(1, 1).wait_recv()

    u = din[...].astype(F32) + hin[...].astype(F32)
    a = normed(u, gd[...], xhat_d, rstd_d, acts_d)

    @pl.when(s > 0)
    def _():
        dout[...] = (u + conv(a, wd)).astype(BF16)
        hop(1, -1).start()
        spread_start(1)

    slope(xhat_d, gd[...], slope_d)

    @pl.when(late)
    def _():
        first_idle()
        spread_wait(1)
        shifted_acts(1)

    @pl.when(s > 0)
    def _():
        hop(2, -1).wait_recv()
        yb = ein[...]
        cots_d[slot] = yb
        ga_s[...] = conv(yb.astype(F32), wd_rev)
        yin[...] = yb

    y = jnp.where(s == 0, loss_scale, 1.0) * yin[...].astype(F32)
    c, gain_cells = backward(ga_s[...], y, gd[...], xhat_d, slope_d, rstd_d)
    skip[...] = c

    @pl.when(s < last)
    def _():
        eout[...] = c.astype(BF16)
        hop(2, 1).start()

    dec_gain_row = cell_sum(gain_cells)

    @pl.when(s == 0)
    def _():
        spread_start(1)

    @pl.when(s > 0)
    def _():
        spread_start(2)

    @pl.when(jnp.logical_not(late))
    def _():
        spread_wait(1)
        shifted_acts(1)
        spread_wait(2)
        dec_weight_grads()

    @pl.when(s < last)
    def _():
        hop(2, 1).wait_send()
        hop(3, 1).wait_recv()

    c = skip[...]
    y = jnp.where(s == last, c, fin[...].astype(F32))
    yb = y.astype(BF16)
    cots_e[slot] = yb
    for j in range(nd - 1, -1, -1):
        near_copy(j, slot).start()
    ga = conv(yb.astype(F32), we_rev)
    f, gain_cells = backward(ga, y, ge[...], xhat_e, slope_e, rstd_e)

    @pl.when(s > 0)
    def _():
        fout[...] = (f + c).astype(BF16)
        hop(3, -1).start()

    enc_gain_row = cell_sum(gain_cells)
    at8 = lax.broadcasted_iota(jnp.int32, (8, channels), 0)
    gains[slot] = jnp.where(at8 == 0, enc_gain_row, jnp.where(at8 == 1, dec_gain_row, 0.0))
    spread_start(4)

    for j in range(1, nd):
        near_copy(j, lax.rem(d - j + nd, nd) * nr + r).wait_recv()
        relay_copy(j, r).start()

    @pl.when(late)
    def _():
        spread_wait(2)
        dec_weight_grads()

    near_copy(0, d * nr + 1 - r).wait_recv()
    add_chip(0, d, True)
    for j in range(1, nd):
        relay_copy(j, 1 - r).wait_recv()
        add_chip(0, lax.rem(d - j + nd, nd), False)
    write_grads(out_we)
    spread_wait(4)
    total = jnp.sum(gains[...], axis=0)
    width = out_ge.shape[1]
    piece = total[:, 0:width]
    for i in range(1, peers):
        piece = jnp.where(me == i, total[:, i * width : (i + 1) * width], piece)
    out_ge[...] = piece[0:1]
    out_gd[...] = piece[1:2]

    @pl.when(s > 0)
    def _():
        hop(1, -1).wait_send()
        hop(3, -1).wait_send()

    for j in range(nd):
        near_copy(j, slot).wait_send()
    for j in range(1, nd):
        relay_copy(j, r).wait_send()


def write_kernel(*refs):
    sources, targets, held, sems = refs[:4], refs[4:8], refs[8:12], refs[12]
    arrive = [pltpu.make_async_copy(sources[i], held[i], sems.at[0, i]) for i in range(4)]
    leave = [pltpu.make_async_copy(held[i], targets[i], sems.at[1, i]) for i in range(4)]
    for c in arrive:
        c.start()
    for c, after in zip(arrive, leave):
        c.wait()
        after.start()
    for c in leave:
        c.wait()


def one_kernel(latent, enc_weight, dec_weight, enc_gain, dec_gain, out_grad):
    batches, frames, rows_here, columns, channels = latent.shape
    ns, nr, nd = (lax.axis_size(a) for a in ("section", "rows", "dp"))
    peers = nr * nd
    cells = frames * rows_here * nr * columns
    counted = cells * (channels // GROUPS)
    loss_scale = 1.0 / math.sqrt(batches * nd * cells)
    taps = 27 * channels
    share = taps // peers
    blocks = max(
        min((i * share + share - 1) // channels, 26) - i * share // channels + 1
        for i in range(peers)
    )
    field = pltpu.VMEM((cells, channels), BF16)
    wide = pltpu.VMEM((cells, channels), F32)
    weights = pltpu.VMEM((taps, channels), BF16)
    turned = pltpu.VMEM((channels, taps), BF16)
    every = pltpu.VMEM((peers, cells, channels), BF16)
    vector = pltpu.VMEM((1, channels), F32)
    vmem = pl.BlockSpec(memory_space=pltpu.VMEM)
    anywhere = pl.BlockSpec(memory_space=pl.ANY)
    far = pl.BlockSpec(memory_space=pltpu.HBM)
    part = pltpu.VMEM(latent.shape, BF16)
    dma = pltpu.SemaphoreType.DMA
    flops = 2 * cells * taps * channels * 4 + 4 * share * peers * cells * channels
    grads = jax.ShapeDtypeStruct((1, channels, share), F32)
    gain_grads = jax.ShapeDtypeStruct((1, channels // peers), F32)
    shapes = (grads, grads, gain_grads, gain_grads)
    results = pl.pallas_call(
        functools.partial(level_kernel, (ns, nr, nd), float(counted), loss_scale, blocks),
        out_shape=shapes,
        in_specs=[far] * 6,
        out_specs=(vmem, vmem, vmem, vmem),
        scratch_shapes=[
            part, part, vector, vector, pltpu.VMEM((channels, channels), BF16),
            turned, turned, weights, weights, weights, weights,
            pltpu.VMEM((2, cells // 2, channels), BF16),
            pltpu.VMEM((2, cells // 2, channels), BF16),
            field, field, field, field, field, field, field, field, field,
            wide, wide, wide, wide, wide, wide, vector, vector,
            every, every, every, every,
            pltpu.VMEM((peers, 8, channels), F32),
            pltpu.VMEM((blocks, channels, peers * cells), BF16),
            pltpu.VMEM((blocks, channels, peers * cells), BF16),
            pltpu.VMEM((blocks * channels, channels), F32),
            dma((2,)), dma((4,)), dma((4,)), dma((4,)), dma((2,)), dma((2,)),
            dma((5, peers)), dma((5, peers)),
        ],
        compiler_params=pltpu.CompilerParams(
            collective_id=0, has_side_effects=True, vmem_limit_bytes=62 * 1024 * 1024
        ),
        cost_estimate=pl.CostEstimate(
            flops=flops, bytes_accessed=4 * taps * channels, transcendentals=4 * cells * channels
        ),
    )(
        latent, out_grad, jnp.swapaxes(enc_weight, 1, 2), jnp.swapaxes(dec_weight, 1, 2),
        enc_gain, dec_gain,
    )
    enc, dec, enc_g, dec_g = pl.pallas_call(
        write_kernel,
        out_shape=shapes,
        in_specs=[anywhere] * 4,
        out_specs=(anywhere,) * 4,
        scratch_shapes=[pltpu.VMEM(x.shape, F32) for x in shapes] + [dma((2, 4))],
        compiler_params=pltpu.CompilerParams(vmem_limit_bytes=62 * 1024 * 1024),
    )(*results)
    return (jnp.swapaxes(enc, 1, 2), jnp.swapaxes(dec, 1, 2), enc_g, dec_g)


def per_device(latent, *rest):
    batches, frames, rows_here, columns, channels = latent.shape
    rows, dp = lax.axis_size("rows"), lax.axis_size("dp")
    taps = 27 * channels
    fits = (
        rows == 2 and batches == 2 and frames == 2 and columns == 8 and rows_here % 4 == 0
        and rows_here * rows * 16 == 128
        and taps % (8 * rows * dp) == 0 and channels % 64 == 0 and channels % (rows * dp) == 0
        and lax.axis_size("section") > 1
    )
    return (one_kernel if fits else on_device)(latent, *rest)


def solution(mesh):
    in_specs = (
        P("dp", None, "rows", None, None),
        P("section", None, None),
        P("section", None, None),
        P("section", None),
        P("section", None),
        P("dp", None, "rows", None, None),
    )
    out_specs = (
        P("section", ("rows", "dp"), None),
        P("section", ("rows", "dp"), None),
        P("section", ("rows", "dp")),
        P("section", ("rows", "dp")),
    )
    return jax.shard_map(
        per_device, mesh=mesh, in_specs=in_specs, out_specs=out_specs, check_vma=False
    )
```
